128 devices in a mesh: space: 8 (over x_hi, z), vel: 16 (over y, x_lo, core).
Axes of the slice: x: 4 (x_hi: 2, x_lo: 2; x = x_hi * 2 + x_lo), y: 4, z: 4, core: 2. Of those that a mesh axis runs over, the one named last changes fastest.
Arguments:
- distribution: float32 [512, 32768], P('space', 'vel'), may hold values from 0.3 to 3
- wall_flags: int32 [512], P('space'), may hold values from 0 to 1, as said below
- cell_slab: int32 [512], P('space'), may hold values from 0 to 15
- species: int32 [512], P('space'), may hold values from 0 to 1
- normal_kernel: float32 [2, 32, 32], replicated, may hold values from 0 to 1, as said below
- tangent_kernel: float32 [2, 32, 32], replicated, may hold values from 0 to 1, as said below
- blow_rate: float32 [16], replicated, may hold values from 0.2 to 2
- emitted: float32 [32768], replicated, may hold values from 0.2 to 2
- spectral: float32 [5, 32768], replicated, may hold values from 0.05 to 1
- collide_rate: float32 [2], replicated, may hold values from 0.3 to 1
Outputs:
- updated: float32 [512, 32768], P('space', 'vel')
The draws below stay inside these ranges and needn't reach their ends.
Inputs may be any that keep to these rules, and one draw needn't show every extreme that they name: `wall_flags`: in each row of 32 cells along the wall normal exactly one cell is flagged, at a normal index below 4. `normal_kernel`: entries are positive. `tangent_kernel`: entries are positive.
All inputs are finite; a program needn't handle non-finite values.
Results may differ from the reference program's by a relative error of at most 0.0003.
Values sent between devices are 32-bit elements; how exact they have to be, the bound alone decides.
A program may use at most 128 MiB of HBM per device.

```python
import math
import jax
import jax.numpy as jnp
from jax import lax

NV = 32
GX = 32
WX = 4
NSPEC = 2
NSEG = 16
PAIRS = 2
GY = 16
CELLS = 512
V = 32768


def draw_wall_flags(key, part):
    depths = jax.random.randint(key, (GY,), 0, WX)
    column = jnp.arange(GX, dtype=jnp.int32)
    return (column[None, :] == depths[:, None]).astype(jnp.int32).reshape(GY * GX)


def draw_normal_kernel(key, part):
    spread = jax.random.uniform(jax.random.fold_in(key, 11), (NSPEC, NV, NV), jnp.float32) * (0.6 / NV)
    mirror = jnp.eye(NV, dtype=jnp.float32)[::-1] * 0.5
    return spread + mirror[None]


def draw_tangent_kernel(key, part):
    spread = jax.random.uniform(jax.random.fold_in(key, 23), (NSPEC, NV, NV), jnp.float32) * (0.6 / NV)
    diagonal = jnp.eye(NV, dtype=jnp.float32) * 0.5
    return spread + diagonal[None]


def touch_ends(array, key, low, top_value):
    index_at = [jax.random.randint(jax.random.fold_in(key, axis), (), 0, length) for axis, length in enumerate(array.shape)]
    longest = array.shape.index(max(array.shape))
    neighbour = index_at[:longest] + [(index_at[longest] + 1) % array.shape[longest]] + index_at[longest + 1:]
    return array.at[tuple(index_at)].set(low).at[tuple(neighbour)].set(top_value)


def steps_of(own_key, dims, cuts, least, top_value):
    gain = 1.0
    for position, shards_of in cuts:
        heights = jax.random.uniform(jax.random.fold_in(jax.random.fold_in(own_key, 6), position), (shards_of,), jnp.float32, least / len(cuts), top_value / len(cuts))
        gain = gain * jnp.repeat(jnp.exp(heights), dims[position] // shards_of).reshape((-1,) + (1,) * (len(dims) - 1 - position))
    return gain


def setup_inputs(seed: int = 0) -> dict:
    splits = jax.random.split(jax.random.key(seed), 11)
    distribution = jnp.clip(jnp.exp(math.log(3.0) - 2.3025851 * jax.random.uniform(splits[0], (CELLS, V), jnp.float32) ** steps_of(splits[0], (CELLS, V), ((0, 8), (1, 16)), -0.2, 0.2)), 0.3, 3.0)
    wall_flags = draw_wall_flags(jax.random.fold_in(splits[10], 71), 0)
    cell_slab = touch_ends(jax.random.randint(splits[2], (CELLS,), 0, NSEG), jax.random.fold_in(splits[2], 1), 0, NSEG - 1).astype(jnp.int32)
    species = touch_ends(jax.random.randint(splits[3], (CELLS,), 0, NSPEC), jax.random.fold_in(splits[3], 1), 0, NSPEC - 1).astype(jnp.int32)
    normal_kernel = draw_normal_kernel(jax.random.fold_in(splits[10], 71), 0)
    tangent_kernel = draw_tangent_kernel(jax.random.fold_in(splits[10], 71), 0)
    blow_rate = jnp.clip(jnp.exp(jax.random.uniform(splits[6], (NSEG,), jnp.float32, math.log(0.2), math.log(2.0))), 0.2, 2.0)
    emitted = jnp.clip(jnp.exp(jax.random.uniform(splits[7], (V,), jnp.float32, math.log(0.2), math.log(2.0))), 0.2, 2.0)
    spectral = jnp.clip(jnp.exp(jax.random.uniform(splits[8], (2 * PAIRS + 1, V), jnp.float32, math.log(0.05), math.log(1.0))), 0.05, 1.0)
    collide_rate = jnp.clip(jnp.exp(jax.random.uniform(splits[9], (NSPEC,), jnp.float32, math.log(0.3), math.log(1.0))), 0.3, 1.0)
    return dict(distribution=distribution, wall_flags=wall_flags, cell_slab=cell_slab, species=species, normal_kernel=normal_kernel, tangent_kernel=tangent_kernel, blow_rate=blow_rate, emitted=emitted, spectral=spectral, collide_rate=collide_rate)


courant = 0.12
top_speed = 4.0
collide_step = 0.5
highest = lax.Precision.HIGHEST


def grid_speed(indices, points):
    return (2.0 * indices.astype(jnp.float32) + 1.0 - points) / points * top_speed


def upwind(values, wall_side, far_side, lower_row, upper_row, normal_nu, along_nu):
    result = values - jnp.maximum(normal_nu, 0.0) * (values - wall_side)
    result = result - jnp.minimum(normal_nu, 0.0) * (far_side - values)
    result = result - jnp.maximum(along_nu, 0.0) * (values - lower_row)
    return result - jnp.minimum(along_nu, 0.0) * (upper_row - values)


def reflect(window, kinds, slab_ids, normal_kernel, tangent_kernel, blow_rate, emitted_part):
    onehot = (kinds[:, None] == jnp.arange(normal_kernel.shape[0])[None, :]).astype(jnp.float32)
    tangent = jnp.einsum("cs,sab->cab", onehot, tangent_kernel, precision=highest)
    normal = jnp.einsum("cs,sab->cab", onehot, normal_kernel, precision=highest)
    turned = jnp.einsum("cab,ckbz->ckaz", tangent, window, precision=highest)
    turned = jnp.einsum("cab,ckyb->ckya", tangent, turned, precision=highest)
    result = jnp.einsum("cok,ckyz->coyz", normal, turned, precision=highest)
    slab_hot = (slab_ids[:, None] == jnp.arange(blow_rate.shape[0])[None, :]).astype(jnp.float32)
    blown = jnp.dot(slab_hot, blow_rate, precision=highest)
    return result + blown[:, None, None, None] * emitted_part[None]


def collide_row(inputs, spectral, collide_rate):
    cell_values, kinds = inputs
    cube = cell_values.reshape(GX, NV, NV, NV)
    spectrum = jnp.fft.fftn(cube, axes=(1, 2, 3))

    def filtered(row):
        weight = spectral[row].reshape(1, NV, NV, NV)
        return jnp.real(jnp.fft.ifftn(spectrum * weight, axes=(1, 2, 3))).astype(jnp.float32)

    gained = jnp.zeros_like(cube)
    for pair in range(PAIRS):
        gained = gained + filtered(pair) * filtered(PAIRS + pair)
    lost_part = cube * filtered(2 * PAIRS)
    onehot = (kinds[:, None] == jnp.arange(NSPEC)[None, :]).astype(jnp.float32)
    rates = jnp.dot(onehot, collide_rate, precision=highest)
    result = cube + collide_step * rates[:, None, None, None] * (gained - lost_part)
    return result.reshape(GX, V)


def reference(distribution, wall_flags, cell_slab, species, normal_kernel, tangent_kernel, blow_rate, emitted, spectral, collide_rate):
    values = distribution.reshape(GY, GX, NV, NV * NV)
    normal_nu = (courant * grid_speed(jnp.arange(NV), NV)).reshape(1, 1, NV, 1)
    along_nu = (courant * grid_speed(jnp.arange(NV * NV) // NV, NV)).reshape(1, 1, 1, NV * NV)
    lower_row = jnp.roll(values, 1, axis=0)
    upper_row = jnp.roll(values, -1, axis=0)
    zero_row = jnp.zeros_like(values[:, :1])
    wall_side = jnp.concatenate([zero_row, values[:, :-1]], axis=1)
    far_side = jnp.concatenate([values[:, 1:], zero_row], axis=1)
    read = upwind(values, wall_side, far_side, lower_row, upper_row, normal_nu, along_nu)
    window = read[:, :WX].reshape(GY * WX, NV, NV, NV)
    kinds = species.reshape(GY, GX)[:, :WX].reshape(GY * WX)
    slab_ids = cell_slab.reshape(GY, GX)[:, :WX].reshape(GY * WX)
    wall_mask = wall_flags.reshape(GY, GX)[:, :WX].reshape(GY * WX)
    reflected = reflect(window, kinds, slab_ids, normal_kernel, tangent_kernel, blow_rate, emitted.reshape(NV, NV, NV))
    window = jnp.where(wall_mask[:, None, None, None] == 1, reflected, window)
    walled = jnp.concatenate([window.reshape(GY, WX, NV, NV * NV), read[:, WX:]], axis=1)
    walled = walled.reshape(GY, GX, V)
    result = lax.map(lambda inputs: collide_row(inputs, spectral, collide_rate), (walled, species.reshape(GY, GX)))
    return result.reshape(CELLS, V)
```

```python
import functools

import jax
import jax.numpy as jnp
import ml_dtypes
import numpy as np
from jax import lax
from jax.experimental import pallas as pl
from jax.experimental.pallas import tpu as pltpu
from jax.sharding import PartitionSpec as P

NV = 32
GX = 32
Q = NV * NV
HALF = Q // 2
OWN = 4
VEL = 16
SPACE = 8
ROWS = NV * OWN
FACTORS = 5
PAIRS = 2
courant = 0.12
top_speed = 4.0
collide_step = 0.5
MESH = pl.DeviceIdType.MESH
f32 = jnp.float32
bf16 = jnp.bfloat16


def parts_of(table):
    hi = table.astype(np.float32).astype(ml_dtypes.bfloat16)
    lo = (table - hi.astype(np.float64)).astype(np.float32).astype(ml_dtypes.bfloat16)
    return hi, lo


def class_slots(parity):
    seen, slots = set(), []
    for kj in range(parity, NV, 2):
        for kl in range(NV):
            other = ((-kj) % NV, (-kl) % NV)
            if other == (kj, kl) or (kj, kl) in seen:
                continue
            seen.add((kj, kl))
            seen.add(other)
            slots.append((kj, kl))
    return slots


def tables():
    j, l = np.divmod(np.arange(HALF), NV)

    def angle(k):
        return 2 * np.pi * ((k[0] * j + k[1] * l) % NV) / NV

    selfs = [((0, 0), (16, 0)), ((0, 16), (16, 16))]
    even, odd = class_slots(0), class_slots(1)
    pair = np.sqrt(2.0) / NV
    t_even = np.zeros((HALF, HALF))
    t_odd = np.zeros((HALF, HALF))
    quarter = HALF // 2
    for n, (a, b) in enumerate(selfs):
        t_even[:, n] = np.cos(angle(a)) / NV
        t_even[:, quarter + n] = np.cos(angle(b)) / NV
    for n, k in enumerate(even):
        t_even[:, n + 2] = pair * np.cos(angle(k))
        t_even[:, quarter + n + 2] = -pair * np.sin(angle(k))
    for n, k in enumerate(odd):
        t_odd[:, n] = pair * np.cos(angle(k))
        t_odd[:, quarter + n] = -pair * np.sin(angle(k))
    big = np.stack(parts_of(t_even) + parts_of(t_odd) + parts_of(t_even.T) + parts_of(t_odd.T))

    phase = 2 * np.pi * (np.outer(np.arange(NV), np.arange(NV)) % NV) / NV
    c = np.kron(np.cos(phase), np.eye(OWN))
    s = np.kron(np.sin(phase), np.eye(OWN))
    fwd = np.block([[c, s], [-s, c]])
    flip = np.block([[c, -s], [-s, -c]])
    inv = np.block([[c, -s], [s, c]])
    left = np.stack(parts_of(fwd) + parts_of(flip) + parts_of(inv))

    w = 0.5 / NV
    width = HALF + 128
    pick = np.zeros((2, Q, width))

    def put(column, k, weight):
        pick[0, k[0] * NV + k[1], column] += weight
        pick[1, ((-k[0]) % NV) * NV + ((-k[1]) % NV), column] += weight

    for n, (a, b) in enumerate(selfs):
        put(n, a, w / 2)
        put(n, b, w / 2)
        put(HALF + n, a, w / 2)
        put(HALF + n, b, -w / 2)
    for n, k in enumerate(even):
        put(n + 2, k, w)
    for n, k in enumerate(odd):
        put(quarter + n, k, w)
    pick = np.concatenate([pick[0], pick[1]], axis=1).astype(ml_dtypes.bfloat16)

    row = np.kron(np.eye(NV), np.ones((OWN, 1)))
    back_row = row[:, (-np.arange(NV)) % NV]
    spread = np.concatenate([row, back_row], axis=1).astype(ml_dtypes.bfloat16)
    row_j = np.kron(np.eye(NV), np.ones((1, NV))).astype(ml_dtypes.bfloat16)
    row_l = np.kron(np.ones((1, NV)), np.eye(NV)).astype(ml_dtypes.bfloat16)
    return big, left, pick, spread, row.astype(ml_dtypes.bfloat16), np.ascontiguousarray(row.T).astype(
        ml_dtypes.bfloat16
    ), np.stack([row_j, row_l])


def split(x):
    hi = x.astype(bf16)
    return hi, (x - hi.astype(f32)).astype(bf16)


def dot(a, b):
    return jnp.dot(a, b, preferred_element_type=f32)


def dot3(x, y):
    return dot(x[0], y[0]) + (dot(x[1], y[0]) + dot(x[0], y[1]))


def kernel(
    x_hbm,
    spectral_hbm,
    big_hbm,
    pick_hbm,
    left,
    spread,
    row_out,
    row_in,
    lanes_in,
    normal,
    tangent,
    emitted,
    flags,
    slabs,
    species,
    blow,
    rates,
    back,
    xv,
    upper,
    lower,
    send,
    recv,
    result,
    big,
    pick,
    spec,
    spec_rows,
    weights,
    weights_self,
    wall_hi,
    wall_lo,
    grid_hi,
    grid_lo,
    local_sem,
    halo_send,
    halo_recv,
    out_send,
    out_recv,
    back_send,
    back_recv,
):
    space = lax.axis_index("space")
    vel = lax.axis_index("vel")
    place_y, place_x, place_c = vel // 4, (vel // 2) % 2, vel % 2
    after, before = (space + 1) % SPACE, (space + SPACE - 1) % SPACE

    def peer(dy, dx, dc):
        return ((place_y + dy) % 4) * 4 + ((place_x + dx) % 2) * 2 + (place_c + dc) % 2

    offsets = [
        (dy, dx, dc)
        for dy in (2, 1, 3, 0)
        for dx in (1, 0)
        for dc in (1, 0)
        if (dy, dx, dc) != (0, 0, 0)
    ]

    load_x = pltpu.make_async_copy(x_hbm, xv, local_sem.at[0])
    load_spec = pltpu.make_async_copy(spectral_hbm, spec, local_sem.at[1])
    load_pick = pltpu.make_async_copy(pick_hbm, pick, local_sem.at[2])
    load_big = pltpu.make_async_copy(big_hbm, big, local_sem.at[3])
    load_x.start()
    load_spec.start()
    load_pick.start()
    load_big.start()

    barrier = pltpu.get_barrier_semaphore()
    for step in range(1, VEL):
        pl.semaphore_signal(
            barrier, inc=1, device_id=(space, (vel + step) % VEL), device_id_type=MESH
        )
    for other in (after, before):
        pl.semaphore_signal(barrier, inc=1, device_id=(other, vel), device_id_type=MESH)
    pl.semaphore_wait(barrier, VEL + 1)

    halos = []
    for own in range(2):
        low = pl.ds(own * Q, HALF)
        high = pl.ds(own * Q + HALF, HALF)
        for number, (src, dst, other) in enumerate(
            (
                (x_hbm.at[pl.ds(0, GX), low], upper, before),
                (x_hbm.at[pl.ds(GX, GX), high], lower, after),
            )
        ):
            copy = pltpu.make_async_remote_copy(
                src_ref=src,
                dst_ref=dst.at[own],
                send_sem=halo_send.at[number, own],
                recv_sem=halo_recv.at[number, own],
                device_id=(other, vel),
                device_id_type=MESH,
            )
            copy.start()
            halos.append(copy)
    load_x.wait()

    lane = lax.broadcasted_iota(jnp.int32, (1, HALF), 1)
    cell = lax.broadcasted_iota(jnp.int32, (GX, HALF), 0)
    sub = lax.broadcasted_iota(jnp.int32, (GX // 8, 8, HALF), 1)

    def speed(index):
        return courant * ((2.0 * index.astype(f32) + 1.0 - NV) / NV * top_speed)

    def upwind(group, half, own, neighbour):
        at = own * Q + half * HALF
        f = xv[group * GX : (group + 1) * GX, at : at + HALF]
        wall_side = jnp.where(cell == 0, 0.0, pltpu.roll(f, 1, 0))
        far_side = jnp.where(cell == GX - 1, 0.0, pltpu.roll(f, GX - 1, 0))
        a = speed(vel * 2 + own)
        b = speed((lane + half * HALF) // NV)
        read = f - jnp.maximum(a, 0.0) * (f - wall_side)
        read = read - jnp.minimum(a, 0.0) * (far_side - f)
        return read - jnp.abs(b) * (f - neighbour)

    def pack(group, half, neighbours):
        r0, r1 = (
            upwind(group, half, own, neighbours[own]).reshape(GX // 8, 8, HALF) for own in range(2)
        )
        first = jnp.where(sub < 4, r0, pltpu.roll(r1, 4, 1))
        second = jnp.where(sub < 4, pltpu.roll(r0, 4, 1), r1)
        lanes = slice(half * HALF, (half + 1) * HALF)
        for m in range(GX // 8):
            send[8 * group + 2 * m, :, lanes] = first[m]
            send[8 * group + 2 * m + 1, :, lanes] = second[m]

    def piece(phase, number, owner, dest):
        half = (dest // 8 + phase) % 2
        lanes = pl.ds(pl.multiple_of(half * HALF, HALF), HALF)
        return pltpu.make_async_remote_copy(
            src_ref=send.at[dest, :, lanes],
            dst_ref=recv.at[owner, :, lanes],
            send_sem=out_send.at[phase, number],
            recv_sem=out_recv.at[phase, owner],
            device_id=(space, dest),
            device_id_type=MESH,
        )

    def send_phase(phase):
        for number, offset in enumerate(offsets):
            piece(phase, number, vel, peer(*offset)).start()

    for group in range(2):
        half = group
        at = half * HALF
        other = slice((1 - group) * GX, (2 - group) * GX)
        pack(group, half, [xv[other, own * Q + at : own * Q + at + HALF] for own in range(2)])
    send_phase(0)

    for copy in halos:
        copy.wait_recv()
    pack(0, 1, [lower[own] for own in range(2)])
    pack(1, 0, [upper[own] for own in range(2)])
    send_phase(1)
    keep = pltpu.make_async_copy(send.at[vel], recv.at[vel], local_sem.at[0])
    keep.start()

    load_spec.wait()
    zero3 = jnp.zeros((8 - FACTORS, Q), f32)
    for k in range(NV):
        spec_rows[k] = jnp.concatenate([spec[:, k * Q : (k + 1) * Q], zero3], axis=0)
    load_pick.wait()
    width = HALF + 128
    for r in range(FACTORS):
        row_hi, row_lo = split(spec_rows[:, r, :])
        both = dot(row_hi, pick[...]) + dot(row_lo, pick[...])
        both = jnp.concatenate([both[:, :width], both[:, width:]], axis=0)
        both_hi, both_lo = split(both)
        whole = dot(spread[...], both_hi) + dot(spread[...], both_lo)
        weights[r] = whole[:, :HALF]
        weights_self[r] = whole[:, HALF:]

    row_id = lax.broadcasted_iota(jnp.int32, (ROWS, 1), 0) % OWN
    first_cell = vel * OWN
    rate_column = jnp.zeros((ROWS, 1), f32)
    for c in range(OWN):
        rate = jnp.where(species[first_cell + c] == 1, rates[1], rates[0])
        rate_column = jnp.where(row_id == c, collide_step * rate, rate_column)

    wall_here = vel % 8 == 0
    kind = 0
    slab = 0
    for c in range(OWN):
        kind = kind + flags[first_cell + c] * species[first_cell + c]
        slab = slab + flags[first_cell + c] * slabs[first_cell + c]

    @pl.when(wall_here)
    def _():
        turn = split(jnp.where(kind == 1, tangent[1], tangent[0]))
        by_j = dot(turn[0], lanes_in[0]) + dot(turn[1], lanes_in[0])
        by_l = dot(turn[0], lanes_in[1]) + dot(turn[1], lanes_in[1])
        for j in range(NV):
            hi, lo = split(by_j[j : j + 1, :] * by_l)
            wall_hi[j * NV : (j + 1) * NV, :] = hi
            wall_lo[j * NV : (j + 1) * NV, :] = lo

    for phase in range(2):
        for offset in offsets:
            piece(phase, 0, peer(*offset), vel).wait_recv()
    keep.wait()

    @pl.when(wall_here)
    def _():
        scatter = split(jnp.where(kind == 1, normal[1], normal[0]))
        wide = split(dot(row_out[...], scatter[0]) + dot(row_out[...], scatter[1]))
        wide = dot(wide[0], row_in[...]) + dot(wide[1], row_in[...])
        same = row_id == lax.broadcasted_iota(jnp.int32, (1, ROWS), 1) % OWN
        wide = split(jnp.where(same, wide, 0.0))
        x = recv[...].reshape(ROWS, Q)
        turned = split(dot3(split(x), (wall_hi[...], wall_lo[...])))
        reflected = dot3(wide, turned)
        gas = jnp.concatenate(
            [emitted[pl.ds(t, NV, stride=Q // 128), :] for t in range(Q // 128)], axis=1
        )
        gas = split(gas)
        gas = dot(row_out[...], gas[0]) + dot(row_out[...], gas[1])
        reflected = reflected + blow[slab] * gas
        flag_column = jnp.zeros((ROWS, 1), jnp.int32)
        for c in range(OWN):
            flag_column = jnp.where(row_id == c, flags[first_cell + c], flag_column)
        recv[...] = jnp.where(flag_column == 1, reflected, x).reshape(VEL, 8, Q)

    load_big.wait()
    quarter = HALF // 2
    xa = recv[:, :, :HALF].reshape(ROWS, HALF)
    xb = recv[:, :, HALF:].reshape(ROWS, HALF)
    ye = dot3(split(xa + xb), (big[0], big[1]))
    yo = dot3(split(xa - xb), (big[2], big[3]))
    z = jnp.concatenate(
        [
            jnp.concatenate([ye[:, :quarter], yo[:, :quarter]], axis=1),
            jnp.concatenate([ye[:, quarter:], yo[:, quarter:]], axis=1),
        ],
        axis=0,
    )
    z = split(z)
    spectrum = dot3((left[0], left[1]), z)
    mirrored = dot3((left[2], left[3]), (z[0][:, :128], z[1][:, :128]))
    for r in range(FACTORS):
        w = jnp.concatenate([weights[r], weights[r]], axis=0)
        d = jnp.concatenate([weights_self[r], weights_self[r]], axis=0)
        scaled = spectrum * w
        first = scaled[:, :128] + mirrored * d
        scaled = split(jnp.concatenate([first, scaled[:, 128:]], axis=1))
        hi, lo = split(dot3((left[4], left[5]), scaled))
        for part, grid in ((hi, grid_hi), (lo, grid_lo)):
            for block in range(2):
                lanes = slice(block * quarter, (block + 1) * quarter)
                grid[block, r, :, :quarter] = part[:ROWS, lanes]
                grid[block, r, :, quarter:] = part[ROWS:, lanes]

    def home(number, dest):
        return pltpu.make_async_remote_copy(
            src_ref=result.at[dest],
            dst_ref=back.at[vel],
            send_sem=back_send.at[number],
            recv_sem=back_recv.at[vel],
            device_id=(space, dest),
            device_id_type=MESH,
        )

    def arrival(owner):
        return pltpu.make_async_remote_copy(
            src_ref=result.at[vel],
            dst_ref=back.at[owner],
            send_sem=back_send.at[0],
            recv_sem=back_recv.at[owner],
            device_id=(space, owner),
            device_id_type=MESH,
        )

    count = ROWS // 4
    rate_part = rate_column[:count]
    for dy in (2, 1, 3, 0):
        plane = (place_y + dy) % 4
        rows = pl.ds(pl.multiple_of(plane * count, count), count)
        sums = []
        for block in range(2):
            lhs = [
                jnp.concatenate([grid[block, r, rows, :] for r in range(FACTORS)], axis=0)
                for grid in (grid_hi, grid_lo)
            ]
            sums.append(dot3(lhs, (big[4 + 2 * block], big[5 + 2 * block])))
        planes = pl.ds(plane * 4, 4)
        for half, total in ((0, sums[0] + sums[1]), (1, sums[0] - sums[1])):
            filtered = [total[r * count : (r + 1) * count] for r in range(FACTORS)]
            walled = recv[planes, :, half * HALF : (half + 1) * HALF].reshape(count, HALF)
            gained = filtered[0] * filtered[2] + filtered[1] * filtered[3]
            updated = walled + rate_part * (gained - walled * filtered[4])
            result[planes, :, half * HALF : (half + 1) * HALF] = updated.reshape(4, 8, HALF)
        for number, offset in enumerate(offsets):
            if offset[0] == dy:
                home(number, peer(*offset)).start()
    keep = pltpu.make_async_copy(result.at[vel], back.at[vel], local_sem.at[0])
    keep.start()

    for copy in halos:
        copy.wait_send()
    for number, offset in enumerate(offsets):
        for phase in range(2):
            piece(phase, number, vel, peer(*offset)).wait_send()
        home(number, peer(*offset)).wait_send()
        arrival(peer(*offset)).wait_recv()
    keep.wait()


def unpack(back, out):
    for m in range(GX // 4):
        first, second = back[2 * m], back[2 * m + 1]
        sub = lax.broadcasted_iota(jnp.int32, (8, Q), 0)
        out[8 * m : 8 * m + 8, :Q] = jnp.where(sub < 4, first, pltpu.roll(second, 4, 0))
        out[8 * m : 8 * m + 8, Q:] = jnp.where(sub < 4, pltpu.roll(first, 4, 0), second)


def on_device(
    distribution,
    wall_flags,
    cell_slab,
    species,
    normal_kernel,
    tangent_kernel,
    blow_rate,
    emitted,
    spectral,
    collide_rate,
):
    big, left, pick, spread, row_out, row_in, lanes_in = tables()
    anywhere = pl.BlockSpec(memory_space=pl.ANY)
    vmem = pl.BlockSpec(memory_space=pltpu.VMEM)
    smem = pl.BlockSpec(memory_space=pltpu.SMEM)
    width = HALF + 128
    dma = pltpu.SemaphoreType.DMA
    back = pl.pallas_call(
        kernel,
        out_shape=jax.ShapeDtypeStruct((VEL, 8, Q), f32),
        in_specs=[anywhere] * 4 + [vmem] * 8 + [smem] * 5,
        out_specs=vmem,
        scratch_shapes=[
            pltpu.VMEM((2 * GX, 2 * Q), f32),
            pltpu.VMEM((2, GX, HALF), f32),
            pltpu.VMEM((2, GX, HALF), f32),
            pltpu.VMEM((VEL, 8, Q), f32),
            pltpu.VMEM((VEL, 8, Q), f32),
            pltpu.VMEM((VEL, 8, Q), f32),
            pltpu.VMEM((8, HALF, HALF), bf16),
            pltpu.VMEM((Q, 2 * width), bf16),
            pltpu.VMEM((FACTORS, NV * Q), f32),
            pltpu.VMEM((NV, 8, Q), f32),
            pltpu.VMEM((FACTORS, ROWS, HALF), f32),
            pltpu.VMEM((FACTORS, ROWS, 128), f32),
            pltpu.VMEM((Q, Q), bf16),
            pltpu.VMEM((Q, Q), bf16),
            pltpu.VMEM((2, FACTORS, ROWS, HALF), bf16),
            pltpu.VMEM((2, FACTORS, ROWS, HALF), bf16),
            dma((4,)),
            dma((2, 2)),
            dma((2, 2)),
            dma((2, VEL)),
            dma((2, VEL)),
            dma((VEL,)),
            dma((VEL,)),
        ],
        compiler_params=pltpu.CompilerParams(
            collective_id=0, has_side_effects=True, vmem_limit_bytes=48 * 2**20
        ),
        name="step",
    )(
        distribution,
        spectral,
        jnp.asarray(big),
        jnp.asarray(pick),
        jnp.asarray(left),
        jnp.asarray(spread),
        jnp.asarray(row_out),
        jnp.asarray(row_in),
        jnp.asarray(lanes_in),
        normal_kernel,
        jnp.swapaxes(tangent_kernel, 1, 2),
        emitted.reshape(NV * Q // 128, 128),
        wall_flags,
        cell_slab,
        species,
        blow_rate,
        collide_rate,
    )
    return pl.pallas_call(
        unpack,
        out_shape=jax.ShapeDtypeStruct((2 * GX, 2 * Q), f32),
        in_specs=[vmem],
        out_specs=vmem,
        name="unpack",
    )(back)


def solution(mesh):
    in_specs = (P("space", "vel"), P("space"), P("space"), P("space"), P(), P(), P(), P(), P(), P())
    out_specs = P("space", "vel")
    return jax.shard_map(
        on_device, mesh=mesh, in_specs=in_specs, out_specs=out_specs, check_vma=False
    )
```

```python
import functools

import jax
import jax.numpy as jnp
import ml_dtypes
import numpy as np
from jax import lax
from jax.experimental import pallas as pl
from jax.experimental.pallas import tpu as pltpu
from jax.sharding import PartitionSpec as P

NV = 32
GX = 32
Q = NV * NV
HALF = Q // 2
OWN = 4
VEL = 16
SPACE = 8
ROWS = NV * OWN
FACTORS = 5
INPUTS = 17
PLACES = 4
courant = 0.12
top_speed = 4.0
collide_step = 0.5
MESH = pl.DeviceIdType.MESH
f32 = jnp.float32
bf16 = jnp.bfloat16


def parts_of(table):
    hi = table.astype(np.float32).astype(ml_dtypes.bfloat16)
    lo = (table - hi.astype(np.float64)).astype(np.float32).astype(ml_dtypes.bfloat16)
    return hi, lo


def class_slots(parity):
    seen, slots = set(), []
    for kj in range(parity, NV, 2):
        for kl in range(NV):
            other = ((-kj) % NV, (-kl) % NV)
            if other == (kj, kl) or (kj, kl) in seen:
                continue
            seen.add((kj, kl))
            seen.add(other)
            slots.append((kj, kl))
    return slots


def tables():
    j, l = np.divmod(np.arange(HALF), NV)

    def angle(k):
        return 2 * np.pi * ((k[0] * j + k[1] * l) % NV) / NV

    selfs = [((0, 0), (16, 0)), ((0, 16), (16, 16))]
    even, odd = class_slots(0), class_slots(1)
    pair = np.sqrt(2.0) / NV
    t_even = np.zeros((HALF, HALF))
    t_odd = np.zeros((HALF, HALF))
    quarter = HALF // 2
    for n, (a, b) in enumerate(selfs):
        t_even[:, n] = np.cos(angle(a)) / NV
        t_even[:, quarter + n] = np.cos(angle(b)) / NV
    for n, k in enumerate(even):
        t_even[:, n + 2] = pair * np.cos(angle(k))
        t_even[:, quarter + n + 2] = -pair * np.sin(angle(k))
    for n, k in enumerate(odd):
        t_odd[:, n] = pair * np.cos(angle(k))
        t_odd[:, quarter + n] = -pair * np.sin(angle(k))
    big = np.stack(parts_of(t_even) + parts_of(t_odd) + parts_of(t_even.T) + parts_of(t_odd.T))

    phase = 2 * np.pi * (np.outer(np.arange(NV), np.arange(NV)) % NV) / NV
    c = np.kron(np.cos(phase), np.eye(OWN))
    s = np.kron(np.sin(phase), np.eye(OWN))
    fwd = np.block([[c, s], [-s, c]])
    flip = np.block([[c, -s], [-s, -c]])
    inv = np.block([[c, -s], [s, c]])
    left = np.stack([np.concatenate(parts_of(t)) for t in (fwd, flip, inv)])

    w = 0.5 / NV
    width = HALF + 128
    pick = np.zeros((2, Q, width))

    def put(column, k, weight):
        pick[0, k[0] * NV + k[1], column] += weight
        pick[1, ((-k[0]) % NV) * NV + ((-k[1]) % NV), column] += weight

    for n, (a, b) in enumerate(selfs):
        put(n, a, w / 2)
        put(n, b, w / 2)
        put(HALF + n, a, w / 2)
        put(HALF + n, b, -w / 2)
    for n, k in enumerate(even):
        put(n + 2, k, w)
    for n, k in enumerate(odd):
        put(quarter + n, k, w)
    pick = np.concatenate([pick[0], pick[1]], axis=1).astype(ml_dtypes.bfloat16)

    row = np.kron(np.eye(NV), np.ones((OWN, 1)))
    back_row = row[:, (-np.arange(NV)) % NV]
    spread = np.concatenate([row, back_row, row, back_row], axis=1).astype(ml_dtypes.bfloat16)
    row_j = np.kron(np.eye(NV), np.ones((1, NV))).astype(ml_dtypes.bfloat16)
    row_l = np.kron(np.ones((1, NV)), np.eye(NV)).astype(ml_dtypes.bfloat16)
    return big, left, pick, spread, row.astype(ml_dtypes.bfloat16), np.ascontiguousarray(row.T).astype(
        ml_dtypes.bfloat16
    ), np.stack([row_j, row_l])


def split(x):
    hi = x.astype(bf16)
    return hi, (x - hi.astype(f32)).astype(bf16)


def dot(a, b):
    return jnp.dot(a, b, preferred_element_type=f32)


def dot_first(a, b):
    return lax.dot_general(a, b, (((0,), (0,)), ((), ())), preferred_element_type=f32)


def right3(x, table_hi, table_lo):
    hi, lo = x
    both = dot(jnp.concatenate([hi, lo], axis=0), table_hi)
    return both[: hi.shape[0]] + (both[hi.shape[0] :] + dot(hi, table_lo))


def left3(table, x):
    count = table.shape[0] // 2
    both = dot(table, x[0])
    return both[:count] + (both[count:] + dot(table[:count], x[1]))


def kernel(*refs):
    given, (back, *scratch) = refs[:INPUTS], refs[INPUTS:]
    x_hbm = given[0]
    held, scratch = scratch[:INPUTS], scratch[INPUTS:]
    (
        xv,
        spec,
        pick,
        big,
        left,
        spread,
        row_out,
        row_in,
        lanes_in,
        normal,
        tangent,
        emitted,
        flags,
        slabs,
        species,
        blow,
        rates,
    ) = held
    (
        upper,
        lower,
        send,
        recv,
        result,
        spec_rows,
        weights,
        weights_self,
        wall_hi,
        wall_lo,
        part,
        grid_hi,
        grid_lo,
        load_sem,
        keep_sem,
        halo_send,
        halo_recv,
        out_send,
        out_recv,
        back_send,
        back_recv,
    ) = scratch
    space = lax.axis_index("space")
    vel = lax.axis_index("vel")
    place_y, place_x, place_c = vel // 4, (vel // 2) % 2, vel % 2
    after, before = (space + 1) % SPACE, (space + SPACE - 1) % SPACE

    def peer(dy, dx, dc):
        return ((place_y + dy) % 4) * 4 + ((place_x + dx) % 2) * 2 + (place_c + dc) % 2

    offsets = [
        (dy, dx, dc)
        for dy in (2, 1, 3, 0)
        for dx in (1, 0)
        for dc in (1, 0)
        if (dy, dx, dc) != (0, 0, 0)
    ]

    loads = [
        pltpu.make_async_copy(src, dst, load_sem.at[n]) for n, (src, dst) in enumerate(zip(given, held))
    ]
    for load in loads:
        load.start()

    barrier = pltpu.get_barrier_semaphore()
    for step in range(1, VEL):
        pl.semaphore_signal(
            barrier, inc=1, device_id=(space, (vel + step) % VEL), device_id_type=MESH
        )
    for other in (after, before):
        pl.semaphore_signal(barrier, inc=1, device_id=(other, vel), device_id_type=MESH)
    pl.semaphore_wait(barrier, VEL + 1)

    chunks = GX // 8
    first_chunk = (place_y * 2 + place_x) % chunks

    def halo(m, own, number):
        rows = pl.multiple_of(m * 8, 8)
        low = x_hbm.at[pl.ds(rows, 8), pl.ds(own * Q, HALF)]
        high = x_hbm.at[pl.ds(GX + rows, 8), pl.ds(own * Q + HALF, HALF)]
        src, dst, other = ((low, upper, before), (high, lower, after))[number]
        return pltpu.make_async_remote_copy(
            src_ref=src,
            dst_ref=dst.at[own, pl.ds(rows, 8)],
            send_sem=halo_send.at[number, own * chunks + m],
            recv_sem=halo_recv.at[number, own * chunks + m],
            device_id=(other, vel),
            device_id_type=MESH,
        )

    for t in range(chunks):
        for own in range(2):
            for number in range(2):
                halo((first_chunk + t) % chunks, own, number).start()
    loads[0].wait()

    lane = lax.broadcasted_iota(jnp.int32, (1, HALF), 1)
    cell = lax.broadcasted_iota(jnp.int32, (GX, HALF), 0)

    def speed(index):
        return courant * ((2.0 * index.astype(f32) + 1.0 - NV) / NV * top_speed)

    def along_normal(group, half, own):
        at = own * Q + half * HALF
        f = xv[group * GX : (group + 1) * GX, at : at + HALF]
        wall_side = jnp.where(cell == 0, 0.0, pltpu.roll(f, 1, 0))
        far_side = jnp.where(cell == GX - 1, 0.0, pltpu.roll(f, GX - 1, 0))
        a = speed(vel * 2 + own)
        read = f - jnp.maximum(a, 0.0) * (f - wall_side)
        return f, read - jnp.minimum(a, 0.0) * (far_side - f)

    def along_wall(half, f, read, neighbour):
        return read - jnp.abs(speed((lane + half * HALF) // NV)) * (f - neighbour)

    def pack(r0, r1):
        r0, r1 = (r.reshape(r.shape[0] // 8, 8, HALF) for r in (r0, r1))
        sub = lax.broadcasted_iota(jnp.int32, r0.shape, 1)
        first = jnp.where(sub < 4, r0, pltpu.roll(r1, 4, 1))
        return first, jnp.where(sub < 4, pltpu.roll(r0, 4, 1), r1)

    def piece(phase, owner, dest):
        half = (dest // 8 + phase) % 2
        lanes = pl.ds(pl.multiple_of(half * HALF, HALF), HALF)
        return pltpu.make_async_remote_copy(
            src_ref=send.at[dest, :, lanes],
            dst_ref=recv.at[owner, :, lanes],
            send_sem=out_send.at[phase, dest],
            recv_sem=out_recv.at[phase, owner],
            device_id=(space, dest),
            device_id_type=MESH,
        )

    for group in range(2):
        half = group
        at = half * HALF
        other = slice((1 - group) * GX, (2 - group) * GX)
        read = []
        for own in range(2):
            f, along = along_normal(group, half, own)
            neighbour = xv[other, own * Q + at : own * Q + at + HALF]
            read.append(along_wall(half, f, along, neighbour))
        first, second = pack(*read)
        for m in range(chunks):
            send[8 * group + 2 * m, :, at : at + HALF] = first[m]
            send[8 * group + 2 * m + 1, :, at : at + HALF] = second[m]
    for offset in offsets:
        piece(0, vel, peer(*offset)).start()

    for group in range(2):
        for own in range(2):
            part[group, own] = along_normal(group, 1 - group, own)[1]
    for load in loads[1:]:
        load.wait()
    zero3 = jnp.zeros((8 - FACTORS, Q), f32)
    for k in range(NV):
        spec_rows[k] = jnp.concatenate([spec[:, k * Q : (k + 1) * Q], zero3], axis=0)
    width = HALF + 128
    rows_hi, rows_lo = split(
        jnp.concatenate([spec_rows[:, r, :] for r in range(FACTORS)], axis=0)
    )
    both = dot(jnp.concatenate([rows_hi, rows_lo], axis=0), pick[...])
    both = split(both[: FACTORS * NV] + both[FACTORS * NV :])
    for r in range(FACTORS):
        pieces = [b[r * NV : (r + 1) * NV, n * width : (n + 1) * width] for b in both for n in range(2)]
        whole = dot(spread[...], jnp.concatenate(pieces, axis=0))
        weights[r] = whole[:, :HALF]
        weights_self[r] = whole[:, HALF:]

    def second_phase(t, carry):
        m = (first_chunk + t) % chunks
        rows = pl.multiple_of(m * 8, 8)
        for own in range(2):
            for number in range(2):
                halo(m, own, number).wait_recv()
        for group in range(2):
            half = 1 - group
            at = half * HALF
            beside = (lower, upper)[group]
            read = []
            for own in range(2):
                f = xv[pl.ds(group * GX + rows, 8), own * Q + at : own * Q + at + HALF]
                along = part[group, own, pl.ds(rows, 8)]
                read.append(along_wall(half, f, along, beside[own, pl.ds(rows, 8)]))
            first, second = pack(*read)
            send[8 * group + 2 * m, :, at : at + HALF] = first[0]
            send[8 * group + 2 * m + 1, :, at : at + HALF] = second[0]
            for n in range(2):
                dest = 8 * group + 2 * m + n

                @pl.when(dest != vel)
                def _():
                    piece(1, vel, dest).start()

        return carry

    lax.fori_loop(0, chunks, second_phase, 0)
    keep = pltpu.make_async_copy(send.at[vel], recv.at[vel], keep_sem.at[0])
    keep.start()

    row_id = lax.broadcasted_iota(jnp.int32, (ROWS, 1), 0) % OWN
    first_cell = vel * OWN
    rate_column = jnp.zeros((ROWS, 1), f32)
    for c in range(OWN):
        rate = jnp.where(species[first_cell + c] == 1, rates[1], rates[0])
        rate_column = jnp.where(row_id == c, collide_step * rate, rate_column)

    wall_here = vel % 8 == 0
    kind = 0
    slab = 0
    for c in range(OWN):
        kind = kind + flags[first_cell + c] * species[first_cell + c]
        slab = slab + flags[first_cell + c] * slabs[first_cell + c]

    @pl.when(wall_here)
    def _():
        turn = split(jnp.where(kind == 1, tangent[1], tangent[0]))
        by_j = dot_first(turn[0], lanes_in[0]) + dot_first(turn[1], lanes_in[0])
        by_l = dot_first(turn[0], lanes_in[1]) + dot_first(turn[1], lanes_in[1])
        for j in range(NV):
            hi, lo = split(by_j[j : j + 1, :] * by_l)
            wall_hi[j * NV : (j + 1) * NV, :] = hi
            wall_lo[j * NV : (j + 1) * NV, :] = lo

    for phase in range(2):
        for offset in offsets:
            piece(phase, peer(*offset), vel).wait_recv()
    keep.wait()

    @pl.when(wall_here)
    def _():
        scatter = split(jnp.where(kind == 1, normal[1], normal[0]))
        wide = split(dot(row_out[...], scatter[0]) + dot(row_out[...], scatter[1]))
        wide = dot(wide[0], row_in[...]) + dot(wide[1], row_in[...])
        same = row_id == lax.broadcasted_iota(jnp.int32, (1, ROWS), 1) % OWN
        wide = split(jnp.where(same, wide, 0.0))
        x = recv[...].reshape(ROWS, Q)
        turned = split(right3(split(x), wall_hi[...], wall_lo[...]))
        reflected = left3(jnp.concatenate(wide, axis=0), turned)
        gas = jnp.concatenate(
            [emitted[pl.ds(t, NV, stride=Q // 128), :] for t in range(Q // 128)], axis=1
        )
        gas = split(gas)
        gas = dot(row_out[...], gas[0]) + dot(row_out[...], gas[1])
        reflected = reflected + blow[slab] * gas
        flag_column = jnp.zeros((ROWS, 1), jnp.int32)
        for c in range(OWN):
            flag_column = jnp.where(row_id == c, flags[first_cell + c], flag_column)
        recv[...] = jnp.where(flag_column == 1, reflected, x).reshape(VEL, 8, Q)

    quarter = HALF // 2
    xa = recv[:, :, :HALF].reshape(ROWS, HALF)
    xb = recv[:, :, HALF:].reshape(ROWS, HALF)
    ye = right3(split(xa + xb), big[0], big[1])
    yo = right3(split(xa - xb), big[2], big[3])
    z = jnp.concatenate(
        [
            jnp.concatenate([ye[:, :quarter], yo[:, :quarter]], axis=1),
            jnp.concatenate([ye[:, quarter:], yo[:, quarter:]], axis=1),
        ],
        axis=0,
    )
    z = split(z)
    spectrum = left3(left[0], z)
    mirrored = left3(left[1], (z[0][:, :128], z[1][:, :128]))
    for r in range(FACTORS):
        w = jnp.concatenate([weights[r], weights[r]], axis=0)
        d = jnp.concatenate([weights_self[r], weights_self[r]], axis=0)
        scaled = spectrum * w
        first = scaled[:, :128] + mirrored * d
        scaled = split(jnp.concatenate([first, scaled[:, 128:]], axis=1))
        hi, lo = split(left3(left[2], scaled))
        for part, grid in ((hi, grid_hi), (lo, grid_lo)):
            for block in range(2):
                lanes = slice(block * quarter, (block + 1) * quarter)
                grid[block, r, :, :quarter] = part[:ROWS, lanes]
                grid[block, r, :, quarter:] = part[ROWS:, lanes]

    def home(number, dest):
        return pltpu.make_async_remote_copy(
            src_ref=result.at[dest],
            dst_ref=back.at[vel],
            send_sem=back_send.at[number],
            recv_sem=back_recv.at[vel],
            device_id=(space, dest),
            device_id_type=MESH,
        )

    def arrival(owner):
        return pltpu.make_async_remote_copy(
            src_ref=result.at[vel],
            dst_ref=back.at[owner],
            send_sem=back_send.at[0],
            recv_sem=back_recv.at[owner],
            device_id=(space, owner),
            device_id_type=MESH,
        )

    count = ROWS // 4
    rate_part = rate_column[:count]
    for dy in (2, 1, 3, 0):
        plane = (place_y + dy) % 4
        rows = pl.ds(pl.multiple_of(plane * count, count), count)
        sums = []
        for block in range(2):
            lhs = [
                jnp.concatenate([grid[block, r, rows, :] for r in range(FACTORS)], axis=0)
                for grid in (grid_hi, grid_lo)
            ]
            sums.append(right3(lhs, big[4 + 2 * block], big[5 + 2 * block]))
        planes = pl.ds(plane * 4, 4)
        for half, total in ((0, sums[0] + sums[1]), (1, sums[0] - sums[1])):
            filtered = [total[r * count : (r + 1) * count] for r in range(FACTORS)]
            walled = recv[planes, :, half * HALF : (half + 1) * HALF].reshape(count, HALF)
            gained = filtered[0] * filtered[2] + filtered[1] * filtered[3]
            updated = walled + rate_part * (gained - walled * filtered[4])
            result[planes, :, half * HALF : (half + 1) * HALF] = updated.reshape(4, 8, HALF)
        for number, offset in enumerate(offsets):
            if offset[0] == dy:
                home(number, peer(*offset)).start()
    keep = pltpu.make_async_copy(result.at[vel], back.at[vel], keep_sem.at[1])
    keep.start()

    for m in range(chunks):
        for own in range(2):
            for number in range(2):
                halo(m, own, number).wait_send()
    for number, offset in enumerate(offsets):
        for phase in range(2):
            piece(phase, vel, peer(*offset)).wait_send()
        home(number, peer(*offset)).wait_send()
        arrival(peer(*offset)).wait_recv()
    keep.wait()


def place(back, out, held, rows, load_sem, store_sem):
    step = VEL // PLACES
    loads, stores = [], []
    for n in range(PLACES):
        owners = pl.ds(n * step, step)
        cells = pl.ds(n * step * OWN, step * OWN)
        loads.append(pltpu.make_async_copy(back.at[owners], held.at[owners], load_sem.at[n]))
        stores.append(pltpu.make_async_copy(rows.at[cells], out.at[cells], store_sem.at[n]))
        loads[n].start()
    sub = lax.broadcasted_iota(jnp.int32, (8, Q), 0)
    for n in range(PLACES):
        loads[n].wait()
        for m in range(n * step // 2, (n + 1) * step // 2):
            first, second = held[2 * m], held[2 * m + 1]
            rows[8 * m : 8 * m + 8, :Q] = jnp.where(sub < 4, first, pltpu.roll(second, 4, 0))
            rows[8 * m : 8 * m + 8, Q:] = jnp.where(sub < 4, pltpu.roll(first, 4, 0), second)
        stores[n].start()
    for store in stores:
        store.wait()


def on_device(
    distribution,
    wall_flags,
    cell_slab,
    species,
    normal_kernel,
    tangent_kernel,
    blow_rate,
    emitted,
    spectral,
    collide_rate,
):
    big, left, pick, spread, row_out, row_in, lanes_in = (jnp.asarray(t) for t in tables())
    dma = pltpu.SemaphoreType.DMA
    in_vmem = [
        distribution,
        spectral,
        pick,
        big,
        left,
        spread,
        row_out,
        row_in,
        lanes_in,
        normal_kernel,
        tangent_kernel,
        emitted.reshape(NV * Q // 128, 128),
    ]
    in_smem = [wall_flags, cell_slab, species, blow_rate, collide_rate]
    back = pl.pallas_call(
        kernel,
        out_shape=jax.ShapeDtypeStruct((VEL, 8, Q), f32),
        in_specs=[pl.BlockSpec(memory_space=pltpu.HBM)] * INPUTS,
        out_specs=pl.BlockSpec(memory_space=pltpu.HBM),
        scratch_shapes=[pltpu.VMEM(x.shape, x.dtype) for x in in_vmem]
        + [pltpu.SMEM(x.shape, x.dtype) for x in in_smem]
        + [
            pltpu.VMEM((2, GX, HALF), f32),
            pltpu.VMEM((2, GX, HALF), f32),
            pltpu.VMEM((VEL, 8, Q), f32),
            pltpu.VMEM((VEL, 8, Q), f32),
            pltpu.VMEM((VEL, 8, Q), f32),
            pltpu.VMEM((NV, 8, Q), f32),
            pltpu.VMEM((FACTORS, ROWS, HALF), f32),
            pltpu.VMEM((FACTORS, ROWS, 128), f32),
            pltpu.VMEM((Q, Q), bf16),
            pltpu.VMEM((Q, Q), bf16),
            pltpu.VMEM((2, 2, GX, HALF), f32),
            pltpu.VMEM((2, FACTORS, ROWS, HALF), bf16),
            pltpu.VMEM((2, FACTORS, ROWS, HALF), bf16),
            dma((INPUTS,)),
            dma((2,)),
            dma((2, 2 * GX // 8)),
            dma((2, 2 * GX // 8)),
            dma((2, VEL)),
            dma((2, VEL)),
            dma((VEL,)),
            dma((VEL,)),
        ],
        compiler_params=pltpu.CompilerParams(
            collective_id=0, has_side_effects=True, vmem_limit_bytes=56 * 2**20
        ),
        name="step",
    )(*in_vmem, *in_smem)
    return pl.pallas_call(
        place,
        out_shape=jax.ShapeDtypeStruct((2 * GX, 2 * Q), f32),
        in_specs=[pl.BlockSpec(memory_space=pltpu.HBM)],
        out_specs=pl.BlockSpec(memory_space=pltpu.HBM),
        scratch_shapes=[
            pltpu.VMEM((VEL, 8, Q), f32),
            pltpu.VMEM((2 * GX, 2 * Q), f32),
            dma((PLACES,)),
            dma((PLACES,)),
        ],
        compiler_params=pltpu.CompilerParams(vmem_limit_bytes=60 * 2**20),
        name="place",
    )(back)


def solution(mesh):
    in_specs = (P("space", "vel"), P("space"), P("space"), P("space"), P(), P(), P(), P(), P(), P())
    out_specs = P("space", "vel")
    return jax.shard_map(
        on_device, mesh=mesh, in_specs=in_specs, out_specs=out_specs, check_vma=False
    )
```

```python
import functools

import jax
import jax.numpy as jnp
import ml_dtypes
import numpy as np
from jax import lax
from jax.experimental import pallas as pl
from jax.experimental.pallas import tpu as pltpu
from jax.sharding import PartitionSpec as P

NV = 32
GX = 32
WX = 4
Q = NV * NV
HALF = Q // 2
BATCHES = 2
OWN = 2
BLOCK = 2 * OWN
VEL = 16
SPACE = 8
ROWS = NV * OWN
FACTORS = 5
INPUTS = 17
courant = 0.12
top_speed = 4.0
collide_step = 0.5
MESH = pl.DeviceIdType.MESH
f32 = jnp.float32
bf16 = jnp.bfloat16


def parts_of(table):
    hi = table.astype(np.float32).astype(ml_dtypes.bfloat16)
    lo = (table - hi.astype(np.float64)).astype(np.float32).astype(ml_dtypes.bfloat16)
    return hi, lo


def class_slots(parity):
    seen, slots = set(), []
    for kj in range(parity, NV, 2):
        for kl in range(NV):
            other = ((-kj) % NV, (-kl) % NV)
            if other == (kj, kl) or (kj, kl) in seen:
                continue
            seen.add((kj, kl))
            seen.add(other)
            slots.append((kj, kl))
    return slots


def tables():
    j, l = np.divmod(np.arange(HALF), NV)

    def angle(k):
        return 2 * np.pi * ((k[0] * j + k[1] * l) % NV) / NV

    selfs = [((0, 0), (16, 0)), ((0, 16), (16, 16))]
    even, odd = class_slots(0), class_slots(1)
    pair = np.sqrt(2.0) / NV
    t_even = np.zeros((HALF, HALF))
    t_odd = np.zeros((HALF, HALF))
    quarter = HALF // 2
    for n, (a, b) in enumerate(selfs):
        t_even[:, n] = np.cos(angle(a)) / NV
        t_even[:, quarter + n] = np.cos(angle(b)) / NV
    for n, k in enumerate(even):
        t_even[:, n + 2] = pair * np.cos(angle(k))
        t_even[:, quarter + n + 2] = -pair * np.sin(angle(k))
    for n, k in enumerate(odd):
        t_odd[:, n] = pair * np.cos(angle(k))
        t_odd[:, quarter + n] = -pair * np.sin(angle(k))
    big = np.stack(parts_of(t_even) + parts_of(t_odd) + parts_of(t_even.T) + parts_of(t_odd.T))

    phase = 2 * np.pi * (np.outer(np.arange(NV), np.arange(NV)) % NV) / NV
    c = np.kron(np.cos(phase), np.eye(OWN))
    s = np.kron(np.sin(phase), np.eye(OWN))
    fwd = np.block([[c, s], [-s, c]])
    flip = np.block([[c, -s], [-s, -c]])
    inv = np.block([[c, -s], [s, c]])
    left = []
    for hi, lo in (parts_of(t) for t in (fwd, flip, inv)):
        left.append(np.block([[hi, hi], [lo, np.zeros_like(lo)]]))
    left = np.stack(left)

    w = 0.5 / NV
    width = HALF + 128
    pick = np.zeros((2, Q, width))

    def put(column, k, weight):
        pick[0, k[0] * NV + k[1], column] += weight
        pick[1, ((-k[0]) % NV) * NV + ((-k[1]) % NV), column] += weight

    for n, (a, b) in enumerate(selfs):
        put(n, a, w / 2)
        put(n, b, w / 2)
        put(HALF + n, a, w / 2)
        put(HALF + n, b, -w / 2)
    for n, k in enumerate(even):
        put(n + 2, k, w)
    for n, k in enumerate(odd):
        put(quarter + n, k, w)
    pick = np.concatenate([pick[0], pick[1]], axis=1).astype(ml_dtypes.bfloat16)

    row = np.kron(np.eye(NV), np.ones((OWN, 1)))
    back_row = row[:, (-np.arange(NV)) % NV]
    spread = np.concatenate([row, back_row, row, back_row], axis=1).astype(ml_dtypes.bfloat16)
    row_j = np.kron(np.eye(NV), np.ones((1, NV))).astype(ml_dtypes.bfloat16)
    row_l = np.kron(np.ones((1, NV)), np.eye(NV)).astype(ml_dtypes.bfloat16)
    return big, left, pick, spread, row.astype(ml_dtypes.bfloat16), np.ascontiguousarray(row.T).astype(
        ml_dtypes.bfloat16
    ), np.stack([row_j, row_l])


def split(x):
    hi = x.astype(bf16)
    return hi, (x - hi.astype(f32)).astype(bf16)


def dot(a, b):
    return jnp.dot(a, b, preferred_element_type=f32)


def dot_first(a, b):
    return lax.dot_general(a, b, (((0,), (0,)), ((), ())), preferred_element_type=f32)


def right3(x, table_hi, table_lo):
    hi, lo = x
    both = dot(jnp.concatenate([hi, lo], axis=0), table_hi)
    return both[: hi.shape[0]] + (both[hi.shape[0] :] + dot(hi, table_lo))


def left3(table, x):
    both = dot(table, jnp.concatenate(x, axis=0))
    count = table.shape[0] // 2
    return both[:count] + both[count:]


def kernel(*refs):
    given, (back, *scratch) = refs[:INPUTS], refs[INPUTS:]
    x_hbm = given[0]
    held, scratch = scratch[:INPUTS], scratch[INPUTS:]
    (
        xv,
        spec,
        pick,
        big,
        left,
        spread,
        row_out,
        row_in,
        lanes_in,
        normal,
        tangent,
        emitted,
        flags,
        slabs,
        species,
        blow,
        rates,
    ) = held
    (
        upper,
        lower,
        send,
        recv,
        result,
        spectrum,
        mirrored,
        spec_rows,
        weights,
        weights_self,
        wall_hi,
        wall_lo,
        part,
        grid_hi,
        grid_lo,
        load_sem,
        keep_sem,
        halo_send,
        halo_recv,
        near_send,
        near_recv,
        out_send,
        out_recv,
        back_send,
        back_recv,
    ) = scratch
    space = lax.axis_index("space")
    vel = lax.axis_index("vel")
    place_y, place_x, place_c = vel // 4, (vel // 2) % 2, vel % 2
    after, before = (space + 1) % SPACE, (space + SPACE - 1) % SPACE

    def peer(dy, dx, dc):
        return ((place_y + dy) % 4) * 4 + ((place_x + dx) % 2) * 2 + (place_c + dc) % 2

    offsets = [
        (dy, dx, dc)
        for dy in (2, 1, 3, 0)
        for dx in (1, 0)
        for dc in (1, 0)
        if (dy, dx, dc) != (0, 0, 0)
    ]

    barrier = pltpu.get_barrier_semaphore()
    for other in (after, before):
        pl.semaphore_signal(barrier, inc=1, device_id=(other, vel), device_id_type=MESH)
    for offset in offsets:
        pl.semaphore_signal(barrier, inc=1, device_id=(space, peer(*offset)), device_id_type=MESH)

    loads = [
        pltpu.make_async_copy(src, dst, load_sem.at[n]) for n, (src, dst) in enumerate(zip(given, held))
    ]
    loads[0].start()
    pl.semaphore_wait(barrier, VEL + 1)

    chunks = GX // 8

    def chunk(step):
        return 2 * (step // 2) + (step + place_y) % 2

    def halo(m, own, number):
        rows = pl.multiple_of(m * 8, 8)
        low = x_hbm.at[pl.ds(rows, 8), pl.ds(own * Q, HALF)]
        high = x_hbm.at[pl.ds(GX + rows, 8), pl.ds(own * Q + HALF, HALF)]
        src, dst, other = ((low, upper, before), (high, lower, after))[number]
        return pltpu.make_async_remote_copy(
            src_ref=src,
            dst_ref=dst.at[own, pl.ds(rows, 8)],
            send_sem=halo_send.at[number, own * chunks + m],
            recv_sem=halo_recv.at[number, own * chunks + m],
            device_id=(other, vel),
            device_id_type=MESH,
        )

    for t in range(chunks):
        for own in range(2):
            for number in range(2):
                halo(chunk(t), own, number).start()
    for load in loads[1:]:
        load.start()
    loads[0].wait()

    lane = lax.broadcasted_iota(jnp.int32, (1, HALF), 1)
    cell = lax.broadcasted_iota(jnp.int32, (GX, HALF), 0)

    def speed(index):
        return courant * ((2.0 * index.astype(f32) + 1.0 - NV) / NV * top_speed)

    def along_normal(group, half, own):
        at = own * Q + half * HALF
        f = xv[group * GX : (group + 1) * GX, at : at + HALF]
        wall_side = jnp.where(cell == 0, 0.0, pltpu.roll(f, 1, 0))
        far_side = jnp.where(cell == GX - 1, 0.0, pltpu.roll(f, GX - 1, 0))
        a = speed(vel * 2 + own)
        read = f - jnp.maximum(a, 0.0) * (f - wall_side)
        return f, read - jnp.minimum(a, 0.0) * (far_side - f)

    def along_wall(half, f, read, neighbour):
        return read - jnp.abs(speed((lane + half * HALF) // NV)) * (f - neighbour)

    def pack(group, m, lanes, r0, r1):
        for k in range(4):
            pair = slice(OWN * k, OWN * k + OWN)
            block = jnp.concatenate([r0[pair], r1[pair]], axis=0)
            send[m // 2, 8 * group + 4 * (m % 2) + k, :, lanes] = block

    def lanes_of(half):
        return pl.ds(pl.multiple_of(half * HALF, HALF), HALF)

    def near(owner, dest):
        lanes = lanes_of(dest // 8)
        return pltpu.make_async_remote_copy(
            src_ref=send.at[:, dest, :, lanes],
            dst_ref=recv.at[:, owner, :, lanes],
            send_sem=near_send.at[dest],
            recv_sem=near_recv.at[owner],
            device_id=(space, dest),
            device_id_type=MESH,
        )

    def far(batch, owner, dest):
        lanes = lanes_of(1 - dest // 8)
        return pltpu.make_async_remote_copy(
            src_ref=send.at[batch, dest, :, lanes],
            dst_ref=recv.at[batch, owner, :, lanes],
            send_sem=out_send.at[batch, dest],
            recv_sem=out_recv.at[batch, owner],
            device_id=(space, dest),
            device_id_type=MESH,
        )

    for group in range(2):
        half = group
        at = half * HALF
        other = slice((1 - group) * GX, (2 - group) * GX)
        read = []
        for own in range(2):
            f, along = along_normal(group, half, own)
            neighbour = xv[other, own * Q + at : own * Q + at + HALF]
            read.append(along_wall(half, f, along, neighbour))
        for m in range(chunks):
            pack(group, m, slice(at, at + HALF), *(r[8 * m : 8 * m + 8] for r in read))
    for offset in offsets:
        near(vel, peer(*offset)).start()

    for group in range(2):
        for own in range(2):
            part[group, own] = along_normal(group, 1 - group, own)[1]
    for load in loads[1:]:
        load.wait()
    zero3 = jnp.zeros((8 - FACTORS, Q), f32)
    for k in range(NV):
        spec_rows[k] = jnp.concatenate([spec[:, k * Q : (k + 1) * Q], zero3], axis=0)
    width = HALF + 128
    rows_hi, rows_lo = split(
        jnp.concatenate([spec_rows[:, r, :] for r in range(FACTORS)], axis=0)
    )
    both = dot(jnp.concatenate([rows_hi, rows_lo], axis=0), pick[...])
    both = split(both[: FACTORS * NV] + both[FACTORS * NV :])
    for r in range(FACTORS):
        pieces = [b[r * NV : (r + 1) * NV, n * width : (n + 1) * width] for b in both for n in range(2)]
        whole = dot(spread[...], jnp.concatenate(pieces, axis=0))
        weights[r] = whole[:, :HALF]
        weights_self[r] = whole[:, HALF:]

    def second_phase(t, carry):
        m = chunk(t)
        rows = pl.multiple_of(m * 8, 8)
        for own in range(2):
            for number in range(2):
                halo(m, own, number).wait_recv()
        for group in range(2):
            half = 1 - group
            at = half * HALF
            beside = (lower, upper)[group]
            read = []
            for own in range(2):
                f = xv[pl.ds(group * GX + rows, 8), own * Q + at : own * Q + at + HALF]
                along = part[group, own, pl.ds(rows, 8)]
                read.append(along_wall(half, f, along, beside[own, pl.ds(rows, 8)]))
            pack(group, m, slice(at, at + HALF), *read)
            for k in range(4):
                dest = 8 * group + 4 * (m % 2) + k

                @pl.when(dest != vel)
                def _():
                    far(m // 2, vel, dest).start()

        return carry

    lax.fori_loop(0, chunks, second_phase, 0)
    keep = pltpu.make_async_copy(send.at[:, vel], recv.at[:, vel], keep_sem.at[0])
    keep.start()

    row_id = lax.broadcasted_iota(jnp.int32, (ROWS, 1), 0) % OWN
    first_cell = (vel // 8) * GX + (vel % 8) * OWN
    wall_here = vel % 8 < WX // OWN
    kind = 0
    slab = 0
    for c in range(OWN):
        kind = kind + flags[first_cell + c] * species[first_cell + c]
        slab = slab + flags[first_cell + c] * slabs[first_cell + c]

    @pl.when(wall_here)
    def _():
        turn = split(jnp.where(kind == 1, tangent[1], tangent[0]))
        by_j = dot_first(turn[0], lanes_in[0]) + dot_first(turn[1], lanes_in[0])
        by_l = dot_first(turn[0], lanes_in[1]) + dot_first(turn[1], lanes_in[1])
        for j in range(NV):
            hi, lo = split(by_j[j : j + 1, :] * by_l)
            wall_hi[j * NV : (j + 1) * NV, :] = hi
            wall_lo[j * NV : (j + 1) * NV, :] = lo

    def home(batch, dest):
        return pltpu.make_async_remote_copy(
            src_ref=result.at[batch, dest],
            dst_ref=back.at[batch, vel],
            send_sem=back_send.at[batch, dest],
            recv_sem=back_recv.at[batch, vel],
            device_id=(space, dest),
            device_id_type=MESH,
        )

    def arrival(batch, owner):
        return pltpu.make_async_remote_copy(
            src_ref=result.at[batch, vel],
            dst_ref=back.at[batch, owner],
            send_sem=back_send.at[batch, owner],
            recv_sem=back_recv.at[batch, owner],
            device_id=(space, owner),
            device_id_type=MESH,
        )

    for offset in offsets:
        near(peer(*offset), vel).wait_recv()
    keep.wait()
    quarter = HALF // 2
    count = ROWS // 2

    def collide(batch, carry):
        for offset in offsets:
            far(batch, peer(*offset), vel).wait_recv()

        @pl.when(jnp.logical_and(wall_here, batch == 0))
        def _():
            scatter = split(jnp.where(kind == 1, normal[1], normal[0]))
            wide = split(dot(row_out[...], scatter[0]) + dot(row_out[...], scatter[1]))
            wide = dot(wide[0], row_in[...]) + dot(wide[1], row_in[...])
            same = row_id == lax.broadcasted_iota(jnp.int32, (1, ROWS), 1) % OWN
            wide = split(jnp.where(same, wide, 0.0))
            x = recv[0].reshape(ROWS, Q)
            turned = split(right3(split(x), wall_hi[...], wall_lo[...]))
            reflected = dot(wide[0], turned[0]) + (dot(wide[1], turned[0]) + dot(wide[0], turned[1]))
            gas = jnp.concatenate(
                [emitted[pl.ds(t, NV, stride=Q // 128), :] for t in range(Q // 128)], axis=1
            )
            gas = split(gas)
            gas = dot(row_out[...], gas[0]) + dot(row_out[...], gas[1])
            reflected = reflected + blow[slab] * gas
            flag_column = jnp.zeros((ROWS, 1), jnp.int32)
            for c in range(OWN):
                flag_column = jnp.where(row_id == c, flags[first_cell + c], flag_column)
            recv[0] = jnp.where(flag_column == 1, reflected, x).reshape(VEL, BLOCK, Q)

        rate_part = jnp.zeros((count, 1), f32)
        for c in range(OWN):
            kind_here = species[first_cell + batch * (GX // BATCHES) + c]
            rate = jnp.where(kind_here == 1, rates[1], rates[0])
            rate_part = jnp.where(row_id[:count] == c, collide_step * rate, rate_part)

        xa = recv[batch, :, :, :HALF].reshape(ROWS, HALF)
        xb = recv[batch, :, :, HALF:].reshape(ROWS, HALF)
        ye = right3(split(xa + xb), big[0], big[1])
        yo = right3(split(xa - xb), big[2], big[3])
        z = jnp.concatenate(
            [
                jnp.concatenate([ye[:, :quarter], yo[:, :quarter]], axis=1),
                jnp.concatenate([ye[:, quarter:], yo[:, quarter:]], axis=1),
            ],
            axis=0,
        )
        z = split(z)
        spectrum[...] = left3(left[0], z)
        mirrored[...] = left3(left[1], (z[0][:, :128], z[1][:, :128]))

        def weigh(r, carry):
            w = jnp.concatenate([weights[r], weights[r]], axis=0)
            d = jnp.concatenate([weights_self[r], weights_self[r]], axis=0)
            scaled = spectrum[...] * w
            first = scaled[:, :128] + mirrored[...] * d
            scaled = split(jnp.concatenate([first, scaled[:, 128:]], axis=1))
            hi, lo = split(left3(left[2], scaled))
            for part_, grid in ((hi, grid_hi), (lo, grid_lo)):
                for block in range(2):
                    lanes = slice(block * quarter, (block + 1) * quarter)
                    grid[block, r, :, :quarter] = part_[:ROWS, lanes]
                    grid[block, r, :, quarter:] = part_[ROWS:, lanes]
            return carry

        for r in range(FACTORS):
            weigh(r, 0)

        def restore(step, carry):
            side = (place_y // 2 + 1 + step) % 2
            rows = pl.ds(pl.multiple_of(side * count, count), count)
            sums = []
            for block in range(2):
                lhs = [
                    jnp.concatenate([grid[block, r, rows, :] for r in range(FACTORS)], axis=0)
                    for grid in (grid_hi, grid_lo)
                ]
                sums.append(right3(lhs, big[4 + 2 * block], big[5 + 2 * block]))
            owners = pl.ds(side * (VEL // 2), VEL // 2)
            for half, total in ((0, sums[0] + sums[1]), (1, sums[0] - sums[1])):
                filtered = [total[r * count : (r + 1) * count] for r in range(FACTORS)]
                lanes = slice(half * HALF, (half + 1) * HALF)
                walled = recv[batch, owners, :, lanes].reshape(count, HALF)
                gained = filtered[0] * filtered[2] + filtered[1] * filtered[3]
                updated = walled + rate_part * (gained - walled * filtered[4])
                result[batch, owners, :, lanes] = updated.reshape(VEL // 2, BLOCK, HALF)
            for plane in range(2):
                for dx in (1, 0):
                    for dc in (1, 0):
                        dest = (side * 2 + (place_y + plane) % 2) * 4
                        dest = dest + ((place_x + dx) % 2) * 2 + (place_c + dc) % 2

                        @pl.when(dest != vel)
                        def _():
                            home(batch, dest).start()

            return carry

        for step in range(2):
            restore(step, 0)
        return carry

    for batch in range(BATCHES):
        collide(batch, 0)
    keep = pltpu.make_async_copy(result.at[:, vel], back.at[:, vel], keep_sem.at[1])
    keep.start()

    for m in range(chunks):
        for own in range(2):
            for number in range(2):
                halo(m, own, number).wait_send()
    for offset in offsets:
        near(vel, peer(*offset)).wait_send()
        for batch in range(BATCHES):
            far(batch, vel, peer(*offset)).wait_send()
            home(batch, peer(*offset)).wait_send()
            arrival(batch, peer(*offset)).wait_recv()
    keep.wait()


def place(back, out, held, rows, load_sem, store_sem):
    loads, stores = [], []
    for n in range(GX // 4):
        group, m = n // 4, n % 4
        owners = (m // 2, pl.ds(8 * group + 4 * (m % 2), 4))
        cells = pl.ds(8 * n, 8)
        loads.append(pltpu.make_async_copy(back.at[owners], held.at[n], load_sem.at[n]))
        stores.append(pltpu.make_async_copy(rows.at[cells], out.at[cells], store_sem.at[n]))
        loads[n].start()
    for n in range(GX // 4):
        loads[n].wait()
        for own in range(2):
            block = [held[n, k, own * OWN : (own + 1) * OWN, :] for k in range(4)]
            rows[8 * n : 8 * n + 8, own * Q : (own + 1) * Q] = jnp.concatenate(block, axis=0)
        stores[n].start()
    for store in stores:
        store.wait()


def on_device(
    distribution,
    wall_flags,
    cell_slab,
    species,
    normal_kernel,
    tangent_kernel,
    blow_rate,
    emitted,
    spectral,
    collide_rate,
):
    big, left, pick, spread, row_out, row_in, lanes_in = (jnp.asarray(t) for t in tables())
    dma = pltpu.SemaphoreType.DMA
    in_vmem = [
        distribution,
        spectral,
        pick,
        big,
        left,
        spread,
        row_out,
        row_in,
        lanes_in,
        normal_kernel,
        tangent_kernel,
        emitted.reshape(NV * Q // 128, 128),
    ]
    in_smem = [wall_flags, cell_slab, species, blow_rate, collide_rate]
    back = pl.pallas_call(
        kernel,
        out_shape=jax.ShapeDtypeStruct((BATCHES, VEL, BLOCK, Q), f32),
        in_specs=[pl.BlockSpec(memory_space=pltpu.HBM)] * INPUTS,
        out_specs=pl.BlockSpec(memory_space=pltpu.HBM),
        scratch_shapes=[pltpu.VMEM(x.shape, x.dtype) for x in in_vmem]
        + [pltpu.SMEM(x.shape, x.dtype) for x in in_smem]
        + [
            pltpu.VMEM((2, GX, HALF), f32),
            pltpu.VMEM((2, GX, HALF), f32),
            pltpu.VMEM((BATCHES, VEL, BLOCK, Q), f32),
            pltpu.VMEM((BATCHES, VEL, BLOCK, Q), f32),
            pltpu.VMEM((BATCHES, VEL, BLOCK, Q), f32),
            pltpu.VMEM((2 * ROWS, HALF), f32),
            pltpu.VMEM((2 * ROWS, 128), f32),
            pltpu.VMEM((NV, 8, Q), f32),
            pltpu.VMEM((FACTORS, ROWS, HALF), f32),
            pltpu.VMEM((FACTORS, ROWS, 128), f32),
            pltpu.VMEM((Q, Q), bf16),
            pltpu.VMEM((Q, Q), bf16),
            pltpu.VMEM((2, 2, GX, HALF), f32),
            pltpu.VMEM((2, FACTORS, ROWS, HALF), bf16),
            pltpu.VMEM((2, FACTORS, ROWS, HALF), bf16),
            dma((INPUTS,)),
            dma((2,)),
            dma((2, 2 * GX // 8)),
            dma((2, 2 * GX // 8)),
            dma((VEL,)),
            dma((VEL,)),
            dma((BATCHES, VEL)),
            dma((BATCHES, VEL)),
            dma((BATCHES, VEL)),
            dma((BATCHES, VEL)),
        ],
        compiler_params=pltpu.CompilerParams(
            collective_id=0, has_side_effects=True, vmem_limit_bytes=56 * 2**20
        ),
        name="step",
    )(*in_vmem, *in_smem)
    return pl.pallas_call(
        place,
        out_shape=jax.ShapeDtypeStruct((2 * GX, 2 * Q), f32),
        in_specs=[pl.BlockSpec(memory_space=pltpu.HBM)],
        out_specs=pl.BlockSpec(memory_space=pltpu.HBM),
        scratch_shapes=[
            pltpu.VMEM((GX // 4, 4, BLOCK, Q), f32),
            pltpu.VMEM((2 * GX, 2 * Q), f32),
            dma((GX // 4,)),
            dma((GX // 4,)),
        ],
        compiler_params=pltpu.CompilerParams(vmem_limit_bytes=60 * 2**20),
        name="place",
    )(back)


def solution(mesh):
    in_specs = (P("space", "vel"), P("space"), P("space"), P("space"), P(), P(), P(), P(), P(), P())
    out_specs = P("space", "vel")
    return jax.shard_map(
        on_device, mesh=mesh, in_specs=in_specs, out_specs=out_specs, check_vma=False
    )
```

```python
import functools

import jax
import jax.numpy as jnp
import ml_dtypes
import numpy as np
from jax import lax
from jax.experimental import pallas as pl
from jax.experimental.pallas import tpu as pltpu
from jax.sharding import PartitionSpec as P

NV = 32
GX = 32
WX = 4
Q = NV * NV
HALF = Q // 2
BATCHES = 2
OWN = 2
BLOCK = 2 * OWN
VEL = 16
SPACE = 8
ROWS = NV * OWN
FACTORS = 5
INPUTS = 18
courant = 0.12
top_speed = 4.0
collide_step = 0.5
MESH = pl.DeviceIdType.MESH
f32 = jnp.float32
bf16 = jnp.bfloat16


def parts_of(table):
    hi = table.astype(np.float32).astype(ml_dtypes.bfloat16)
    lo = (table - hi.astype(np.float64)).astype(np.float32).astype(ml_dtypes.bfloat16)
    return hi, lo


def class_slots(first, step):
    seen, slots = set(), []
    for kj in range(first, NV, step):
        for kl in range(NV):
            other = ((-kj) % NV, (-kl) % NV)
            if other == (kj, kl) or (kj, kl) in seen:
                continue
            seen.add((kj, kl))
            seen.add(other)
            slots.append((kj, kl))
    return slots


def tables():
    j, l = np.divmod(np.arange(HALF), NV)

    def angle(k):
        return 2 * np.pi * ((k[0] * j + k[1] * l) % NV) / NV

    selfs = [((0, 0), (16, 0)), ((0, 16), (16, 16))]
    zero, two, odd = class_slots(0, 4), class_slots(2, 4), class_slots(1, 2)
    pair = np.sqrt(2.0) / NV
    quarter = HALF // 2
    eighth = quarter // 2
    t_zero = np.zeros((HALF, quarter))
    t_two = np.zeros((HALF, quarter))
    t_odd = np.zeros((HALF, HALF))
    for n, (a, b) in enumerate(selfs):
        t_zero[:, n] = np.cos(angle(a)) / NV
        t_zero[:, eighth + n] = np.cos(angle(b)) / NV
    for n, k in enumerate(zero):
        t_zero[:, n + 2] = pair * np.cos(angle(k))
        t_zero[:, eighth + n + 2] = -pair * np.sin(angle(k))
    for n, k in enumerate(two):
        t_two[:, n] = pair * np.cos(angle(k))
        t_two[:, eighth + n] = -pair * np.sin(angle(k))
    for n, k in enumerate(odd):
        t_odd[:, n] = pair * np.cos(angle(k))
        t_odd[:, quarter + n] = -pair * np.sin(angle(k))
    t_zero, t_two = t_zero[:quarter], t_two[:quarter]
    big = np.stack(parts_of(t_odd) + parts_of(t_odd.T))
    small = np.stack(
        parts_of(t_zero) + parts_of(t_two) + parts_of(t_zero.T) + parts_of(t_two.T)
    )

    phase = 2 * np.pi * (np.outer(np.arange(NV), np.arange(NV)) % NV) / NV
    c = np.kron(np.cos(phase), np.eye(OWN))
    s = np.kron(np.sin(phase), np.eye(OWN))
    fwd = np.block([[c, s], [-s, c]])
    flip = np.block([[c, -s], [-s, -c]])
    inv = np.block([[c, -s], [s, c]])
    left = []
    for hi, lo in (parts_of(t) for t in (fwd, flip, inv)):
        left.append(np.block([[hi, hi], [lo, np.zeros_like(lo)]]))
    left = np.stack(left)

    w = 0.5 / NV
    width = HALF + 128
    pick = np.zeros((2, Q, width))

    def put(column, k, weight):
        pick[0, k[0] * NV + k[1], column] += weight
        pick[1, ((-k[0]) % NV) * NV + ((-k[1]) % NV), column] += weight

    for n, (a, b) in enumerate(selfs):
        put(n, a, w / 2)
        put(n, b, w / 2)
        put(HALF + n, a, w / 2)
        put(HALF + n, b, -w / 2)
    for n, k in enumerate(zero):
        put(n + 2, k, w)
    for n, k in enumerate(two):
        put(eighth + n, k, w)
    for n, k in enumerate(odd):
        put(quarter + n, k, w)
    pick = np.concatenate([pick[0], pick[1]], axis=1).astype(ml_dtypes.bfloat16)

    row = np.kron(np.eye(NV), np.ones((OWN, 1)))
    back_row = row[:, (-np.arange(NV)) % NV]
    spread = np.concatenate([row, back_row, row, back_row], axis=1).astype(ml_dtypes.bfloat16)
    row_j = np.kron(np.eye(NV), np.ones((1, NV))).astype(ml_dtypes.bfloat16)
    row_l = np.kron(np.ones((1, NV)), np.eye(NV)).astype(ml_dtypes.bfloat16)
    return big, small, left, pick, spread, row.astype(ml_dtypes.bfloat16), np.ascontiguousarray(row.T).astype(
        ml_dtypes.bfloat16
    ), np.stack([row_j, row_l])


def split(x):
    hi = x.astype(bf16)
    return hi, (x - hi.astype(f32)).astype(bf16)


def dot(a, b):
    return jnp.dot(a, b, preferred_element_type=f32)


def dot_first(a, b):
    return lax.dot_general(a, b, (((0,), (0,)), ((), ())), preferred_element_type=f32)


def right3(x, table_hi, table_lo):
    hi, lo = x
    both = dot(jnp.concatenate([hi, lo], axis=0), table_hi)
    return both[: hi.shape[0]] + (both[hi.shape[0] :] + dot(hi, table_lo))


def left3(table, x):
    both = dot(table, jnp.concatenate(x, axis=0))
    count = table.shape[0] // 2
    return both[:count] + both[count:]


def kernel(*refs):
    given, (back, *scratch) = refs[:INPUTS], refs[INPUTS:]
    x_hbm = given[0]
    held, scratch = scratch[:INPUTS], scratch[INPUTS:]
    (
        xv,
        spec,
        pick,
        big,
        small,
        left,
        spread,
        row_out,
        row_in,
        lanes_in,
        normal,
        tangent,
        emitted,
        flags,
        slabs,
        species,
        blow,
        rates,
    ) = held
    (
        upper,
        lower,
        send,
        recv,
        result,
        spectrum,
        mirrored,
        spec_rows,
        weights,
        weights_self,
        wall_hi,
        wall_lo,
        part,
        grid_hi,
        grid_lo,
        load_sem,
        keep_sem,
        halo_send,
        halo_recv,
        near_send,
        near_recv,
        out_send,
        out_recv,
        back_send,
        back_recv,
    ) = scratch
    space = lax.axis_index("space")
    vel = lax.axis_index("vel")
    place_y, place_x, place_c = vel // 4, (vel // 2) % 2, vel % 2
    after, before = (space + 1) % SPACE, (space + SPACE - 1) % SPACE

    def peer(dy, dx, dc):
        return ((place_y + dy) % 4) * 4 + ((place_x + dx) % 2) * 2 + (place_c + dc) % 2

    offsets = [
        (dy, dx, dc)
        for dy in (2, 1, 3, 0)
        for dx in (1, 0)
        for dc in (1, 0)
        if (dy, dx, dc) != (0, 0, 0)
    ]

    barrier = pltpu.get_barrier_semaphore()
    for other in (after, before):
        pl.semaphore_signal(barrier, inc=1, device_id=(other, vel), device_id_type=MESH)
    for offset in offsets:
        pl.semaphore_signal(barrier, inc=1, device_id=(space, peer(*offset)), device_id_type=MESH)

    loads = [
        pltpu.make_async_copy(src, dst, load_sem.at[n]) for n, (src, dst) in enumerate(zip(given, held))
    ]
    loads[0].start()
    pl.semaphore_wait(barrier, VEL + 1)

    chunks = GX // 8

    def chunk(step):
        return 2 * (step // 2) + (step + place_y) % 2

    def halo(m, own, number):
        rows = pl.multiple_of(m * 8, 8)
        low = x_hbm.at[pl.ds(rows, 8), pl.ds(own * Q, HALF)]
        high = x_hbm.at[pl.ds(GX + rows, 8), pl.ds(own * Q + HALF, HALF)]
        src, dst, other = ((low, upper, before), (high, lower, after))[number]
        return pltpu.make_async_remote_copy(
            src_ref=src,
            dst_ref=dst.at[own, pl.ds(rows, 8)],
            send_sem=halo_send.at[number, own * chunks + m],
            recv_sem=halo_recv.at[number, own * chunks + m],
            device_id=(other, vel),
            device_id_type=MESH,
        )

    for t in range(chunks):
        for own in range(2):
            for number in range(2):
                halo(chunk(t), own, number).start()
    for load in loads[1:]:
        load.start()
    loads[0].wait()

    lane = lax.broadcasted_iota(jnp.int32, (1, HALF), 1)
    cell = lax.broadcasted_iota(jnp.int32, (GX, HALF), 0)

    def speed(index):
        return courant * ((2.0 * index.astype(f32) + 1.0 - NV) / NV * top_speed)

    def along_normal(group, half, own):
        at = own * Q + half * HALF
        f = xv[group * GX : (group + 1) * GX, at : at + HALF]
        wall_side = jnp.where(cell == 0, 0.0, pltpu.roll(f, 1, 0))
        far_side = jnp.where(cell == GX - 1, 0.0, pltpu.roll(f, GX - 1, 0))
        a = speed(vel * 2 + own)
        read = f - jnp.maximum(a, 0.0) * (f - wall_side)
        return f, read - jnp.minimum(a, 0.0) * (far_side - f)

    def along_wall(half, f, read, neighbour):
        return read - jnp.abs(speed((lane + half * HALF) // NV)) * (f - neighbour)

    def pack(group, m, lanes, r0, r1):
        for k in range(4):
            pair = slice(OWN * k, OWN * k + OWN)
            block = jnp.concatenate([r0[pair], r1[pair]], axis=0)
            send[m // 2, 8 * group + 4 * (m % 2) + k, :, lanes] = block

    def lanes_of(half):
        return pl.ds(pl.multiple_of(half * HALF, HALF), HALF)

    def near(owner, dest):
        lanes = lanes_of(dest // 8)
        return pltpu.make_async_remote_copy(
            src_ref=send.at[:, dest, :, lanes],
            dst_ref=recv.at[:, owner, :, lanes],
            send_sem=near_send.at[dest],
            recv_sem=near_recv.at[owner],
            device_id=(space, dest),
            device_id_type=MESH,
        )

    def far(batch, owner, dest):
        lanes = lanes_of(1 - dest // 8)
        return pltpu.make_async_remote_copy(
            src_ref=send.at[batch, dest, :, lanes],
            dst_ref=recv.at[batch, owner, :, lanes],
            send_sem=out_send.at[batch, dest],
            recv_sem=out_recv.at[batch, owner],
            device_id=(space, dest),
            device_id_type=MESH,
        )

    for group in range(2):
        half = group
        at = half * HALF
        other = slice((1 - group) * GX, (2 - group) * GX)
        read = []
        for own in range(2):
            f, along = along_normal(group, half, own)
            neighbour = xv[other, own * Q + at : own * Q + at + HALF]
            read.append(along_wall(half, f, along, neighbour))
        for m in range(chunks):
            pack(group, m, slice(at, at + HALF), *(r[8 * m : 8 * m + 8] for r in read))
    for offset in offsets:
        near(vel, peer(*offset)).start()

    for group in range(2):
        for own in range(2):
            part[group, own] = along_normal(group, 1 - group, own)[1]
    for load in loads[1:]:
        load.wait()
    zero3 = jnp.zeros((8 - FACTORS, Q), f32)
    for k in range(NV):
        spec_rows[k] = jnp.concatenate([spec[:, k * Q : (k + 1) * Q], zero3], axis=0)
    width = HALF + 128
    rows_hi, rows_lo = split(
        jnp.concatenate([spec_rows[:, r, :] for r in range(FACTORS)], axis=0)
    )
    both = dot(jnp.concatenate([rows_hi, rows_lo], axis=0), pick[...])
    both = split(both[: FACTORS * NV] + both[FACTORS * NV :])
    for r in range(FACTORS):
        pieces = [b[r * NV : (r + 1) * NV, n * width : (n + 1) * width] for b in both for n in range(2)]
        whole = dot(spread[...], jnp.concatenate(pieces, axis=0))
        weights[r] = whole[:, :HALF]
        weights_self[r] = whole[:, HALF:]

    def second_phase(t, carry):
        m = chunk(t)
        rows = pl.multiple_of(m * 8, 8)
        for own in range(2):
            for number in range(2):
                halo(m, own, number).wait_recv()
        for group in range(2):
            half = 1 - group
            at = half * HALF
            beside = (lower, upper)[group]
            read = []
            for own in range(2):
                f = xv[pl.ds(group * GX + rows, 8), own * Q + at : own * Q + at + HALF]
                along = part[group, own, pl.ds(rows, 8)]
                read.append(along_wall(half, f, along, beside[own, pl.ds(rows, 8)]))
            pack(group, m, slice(at, at + HALF), *read)
            for dx, dc in ((1, 1), (1, 0), (0, 1), (0, 0)):
                k = ((place_x + dx) % 2) * 2 + (place_c + dc) % 2
                dest = 8 * group + 4 * (m % 2) + k

                @pl.when(dest != vel)
                def _():
                    far(m // 2, vel, dest).start()

        return carry

    lax.fori_loop(0, chunks, second_phase, 0)
    keep = pltpu.make_async_copy(send.at[:, vel], recv.at[:, vel], keep_sem.at[0])
    keep.start()

    row_id = lax.broadcasted_iota(jnp.int32, (ROWS, 1), 0) % OWN
    first_cell = (vel // 8) * GX + (vel % 8) * OWN
    wall_here = vel % 8 < WX // OWN
    kind = 0
    slab = 0
    for c in range(OWN):
        kind = kind + flags[first_cell + c] * species[first_cell + c]
        slab = slab + flags[first_cell + c] * slabs[first_cell + c]

    @pl.when(wall_here)
    def _():
        turn = split(jnp.where(kind == 1, tangent[1], tangent[0]))
        by_j = dot_first(turn[0], lanes_in[0]) + dot_first(turn[1], lanes_in[0])
        by_l = dot_first(turn[0], lanes_in[1]) + dot_first(turn[1], lanes_in[1])
        for j in range(NV):
            hi, lo = split(by_j[j : j + 1, :] * by_l)
            wall_hi[j * NV : (j + 1) * NV, :] = hi
            wall_lo[j * NV : (j + 1) * NV, :] = lo

    def home(batch, dest):
        return pltpu.make_async_remote_copy(
            src_ref=result.at[batch, dest],
            dst_ref=back.at[batch, vel],
            send_sem=back_send.at[batch, dest],
            recv_sem=back_recv.at[batch, vel],
            device_id=(space, dest),
            device_id_type=MESH,
        )

    def arrival(batch, owner):
        return pltpu.make_async_remote_copy(
            src_ref=result.at[batch, vel],
            dst_ref=back.at[batch, owner],
            send_sem=back_send.at[batch, owner],
            recv_sem=back_recv.at[batch, owner],
            device_id=(space, owner),
            device_id_type=MESH,
        )

    for offset in offsets:
        near(peer(*offset), vel).wait_recv()
    keep.wait()
    quarter = HALF // 2
    eighth = quarter // 2
    count = ROWS // 2

    def collide(batch, carry):
        for offset in offsets:
            far(batch, peer(*offset), vel).wait_recv()

        @pl.when(jnp.logical_and(wall_here, batch == 0))
        def _():
            scatter = split(jnp.where(kind == 1, normal[1], normal[0]))
            wide = split(dot(row_out[...], scatter[0]) + dot(row_out[...], scatter[1]))
            wide = dot(wide[0], row_in[...]) + dot(wide[1], row_in[...])
            same = row_id == lax.broadcasted_iota(jnp.int32, (1, ROWS), 1) % OWN
            wide = split(jnp.where(same, wide, 0.0))
            x = recv[0].reshape(ROWS, Q)
            turned = split(right3(split(x), wall_hi[...], wall_lo[...]))
            reflected = dot(wide[0], turned[0]) + (dot(wide[1], turned[0]) + dot(wide[0], turned[1]))
            gas = jnp.concatenate(
                [emitted[pl.ds(t, NV, stride=Q // 128), :] for t in range(Q // 128)], axis=1
            )
            gas = split(gas)
            gas = dot(row_out[...], gas[0]) + dot(row_out[...], gas[1])
            reflected = reflected + blow[slab] * gas
            flag_column = jnp.zeros((ROWS, 1), jnp.int32)
            for c in range(OWN):
                flag_column = jnp.where(row_id == c, flags[first_cell + c], flag_column)
            recv[0] = jnp.where(flag_column == 1, reflected, x).reshape(VEL, BLOCK, Q)

        rate_part = jnp.zeros((count, 1), f32)
        for c in range(OWN):
            kind_here = species[first_cell + batch * (GX // BATCHES) + c]
            rate = jnp.where(kind_here == 1, rates[1], rates[0])
            rate_part = jnp.where(row_id[:count] == c, collide_step * rate, rate_part)

        xa = recv[batch, :, :, :HALF].reshape(ROWS, HALF)
        xb = recv[batch, :, :, HALF:].reshape(ROWS, HALF)
        even = xa + xb
        low, high = even[:, :quarter], even[:, quarter:]
        y0 = right3(split(low + high), small[0], small[1])
        y2 = right3(split(low - high), small[2], small[3])
        yo = right3(split(xa - xb), big[0], big[1])
        z = jnp.concatenate(
            [
                jnp.concatenate([y0[:, :eighth], y2[:, :eighth], yo[:, :quarter]], axis=1),
                jnp.concatenate([y0[:, eighth:], y2[:, eighth:], yo[:, quarter:]], axis=1),
            ],
            axis=0,
        )
        z = split(z)
        spectrum[...] = left3(left[0], z)
        mirrored[...] = left3(left[1], (z[0][:, :128], z[1][:, :128]))

        def weigh(r, carry):
            w = jnp.concatenate([weights[r], weights[r]], axis=0)
            d = jnp.concatenate([weights_self[r], weights_self[r]], axis=0)
            scaled = spectrum[...] * w
            first = scaled[:, :128] + mirrored[...] * d
            scaled = split(jnp.concatenate([first, scaled[:, 128:]], axis=1))
            hi, lo = split(left3(left[2], scaled))
            for part_, grid in ((hi, grid_hi), (lo, grid_lo)):
                for n in range(2):
                    lanes = slice(n * eighth, (n + 1) * eighth)
                    grid[0, r, :, n * quarter : n * quarter + eighth] = part_[:ROWS, lanes]
                    grid[0, r, :, n * quarter + eighth : (n + 1) * quarter] = part_[ROWS:, lanes]
                grid[1, r, :, :quarter] = part_[:ROWS, quarter:]
                grid[1, r, :, quarter:] = part_[ROWS:, quarter:]
            return carry

        for r in range(FACTORS):
            weigh(r, 0)

        def restore(step, carry):
            side = (place_y // 2 + 1 + step) % 2
            rows = pl.ds(pl.multiple_of(side * count, count), count)
            def rows_of(block, lanes):
                return [
                    jnp.concatenate([grid[block, r, rows, lanes] for r in range(FACTORS)], axis=0)
                    for grid in (grid_hi, grid_lo)
                ]

            e0 = right3(rows_of(0, slice(0, quarter)), small[4], small[5])
            e2 = right3(rows_of(0, slice(quarter, HALF)), small[6], small[7])
            even = jnp.concatenate([e0 + e2, e0 - e2], axis=1)
            odd = right3(rows_of(1, slice(0, HALF)), big[2], big[3])
            owners = pl.ds(side * (VEL // 2), VEL // 2)
            for half, total in ((0, even + odd), (1, even - odd)):
                filtered = [total[r * count : (r + 1) * count] for r in range(FACTORS)]
                lanes = slice(half * HALF, (half + 1) * HALF)
                walled = recv[batch, owners, :, lanes].reshape(count, HALF)
                gained = filtered[0] * filtered[2] + filtered[1] * filtered[3]
                updated = walled + rate_part * (gained - walled * filtered[4])
                result[batch, owners, :, lanes] = updated.reshape(VEL // 2, BLOCK, HALF)
            for plane in range(2):
                for dx in (1, 0):
                    for dc in (1, 0):
                        dest = (side * 2 + (place_y + plane) % 2) * 4
                        dest = dest + ((place_x + dx) % 2) * 2 + (place_c + dc) % 2

                        @pl.when(dest != vel)
                        def _():
                            home(batch, dest).start()

            return carry

        for step in range(2):
            restore(step, 0)
        return carry

    for batch in range(BATCHES):
        collide(batch, 0)
    keep = pltpu.make_async_copy(result.at[:, vel], back.at[:, vel], keep_sem.at[1])
    keep.start()

    for m in range(chunks):
        for own in range(2):
            for number in range(2):
                halo(m, own, number).wait_send()
    for offset in offsets:
        near(vel, peer(*offset)).wait_send()
        for batch in range(BATCHES):
            far(batch, vel, peer(*offset)).wait_send()
            home(batch, peer(*offset)).wait_send()
            arrival(batch, peer(*offset)).wait_recv()
    keep.wait()


def place(back, out, held, rows, load_sem, store_sem):
    loads, stores = [], []
    for n in range(GX // 4):
        group, m = n // 4, n % 4
        owners = (m // 2, pl.ds(8 * group + 4 * (m % 2), 4))
        cells = pl.ds(8 * n, 8)
        loads.append(pltpu.make_async_copy(back.at[owners], held.at[n], load_sem.at[n]))
        stores.append(pltpu.make_async_copy(rows.at[cells], out.at[cells], store_sem.at[n]))
        loads[n].start()
    for n in range(GX // 4):
        loads[n].wait()
        for own in range(2):
            block = [held[n, k, own * OWN : (own + 1) * OWN, :] for k in range(4)]
            rows[8 * n : 8 * n + 8, own * Q : (own + 1) * Q] = jnp.concatenate(block, axis=0)
        stores[n].start()
    for store in stores:
        store.wait()


def on_device(
    distribution,
    wall_flags,
    cell_slab,
    species,
    normal_kernel,
    tangent_kernel,
    blow_rate,
    emitted,
    spectral,
    collide_rate,
):
    big, small, left, pick, spread, row_out, row_in, lanes_in = (jnp.asarray(t) for t in tables())
    dma = pltpu.SemaphoreType.DMA
    in_vmem = [
        distribution,
        spectral,
        pick,
        big,
        small,
        left,
        spread,
        row_out,
        row_in,
        lanes_in,
        normal_kernel,
        tangent_kernel,
        emitted.reshape(NV * Q // 128, 128),
    ]
    in_smem = [wall_flags, cell_slab, species, blow_rate, collide_rate]
    back = pl.pallas_call(
        kernel,
        out_shape=jax.ShapeDtypeStruct((BATCHES, VEL, BLOCK, Q), f32),
        in_specs=[pl.BlockSpec(memory_space=pltpu.HBM)] * INPUTS,
        out_specs=pl.BlockSpec(memory_space=pltpu.HBM),
        scratch_shapes=[pltpu.VMEM(x.shape, x.dtype) for x in in_vmem]
        + [pltpu.SMEM(x.shape, x.dtype) for x in in_smem]
        + [
            pltpu.VMEM((2, GX, HALF), f32),
            pltpu.VMEM((2, GX, HALF), f32),
            pltpu.VMEM((BATCHES, VEL, BLOCK, Q), f32),
            pltpu.VMEM((BATCHES, VEL, BLOCK, Q), f32),
            pltpu.VMEM((BATCHES, VEL, BLOCK, Q), f32),
            pltpu.VMEM((2 * ROWS, HALF), f32),
            pltpu.VMEM((2 * ROWS, 128), f32),
            pltpu.VMEM((NV, 8, Q), f32),
            pltpu.VMEM((FACTORS, ROWS, HALF), f32),
            pltpu.VMEM((FACTORS, ROWS, 128), f32),
            pltpu.VMEM((Q, Q), bf16),
            pltpu.VMEM((Q, Q), bf16),
            pltpu.VMEM((2, 2, GX, HALF), f32),
            pltpu.VMEM((2, FACTORS, ROWS, HALF), bf16),
            pltpu.VMEM((2, FACTORS, ROWS, HALF), bf16),
            dma((INPUTS,)),
            dma((2,)),
            dma((2, 2 * GX // 8)),
            dma((2, 2 * GX // 8)),
            dma((VEL,)),
            dma((VEL,)),
            dma((BATCHES, VEL)),
            dma((BATCHES, VEL)),
            dma((BATCHES, VEL)),
            dma((BATCHES, VEL)),
        ],
        compiler_params=pltpu.CompilerParams(
            collective_id=0, has_side_effects=True, vmem_limit_bytes=56 * 2**20
        ),
        name="step",
    )(*in_vmem, *in_smem)
    return pl.pallas_call(
        place,
        out_shape=jax.ShapeDtypeStruct((2 * GX, 2 * Q), f32),
        in_specs=[pl.BlockSpec(memory_space=pltpu.HBM)],
        out_specs=pl.BlockSpec(memory_space=pltpu.HBM),
        scratch_shapes=[
            pltpu.VMEM((GX // 4, 4, BLOCK, Q), f32),
            pltpu.VMEM((2 * GX, 2 * Q), f32),
            dma((GX // 4,)),
            dma((GX // 4,)),
        ],
        compiler_params=pltpu.CompilerParams(vmem_limit_bytes=60 * 2**20),
        name="place",
    )(back)


def solution(mesh):
    in_specs = (P("space", "vel"), P("space"), P("space"), P("space"), P(), P(), P(), P(), P(), P())
    out_specs = P("space", "vel")
    return jax.shard_map(
        on_device, mesh=mesh, in_specs=in_specs, out_specs=out_specs, check_vma=False
    )
```

```python
import functools

import jax
import jax.numpy as jnp
import ml_dtypes
import numpy as np
from jax import lax
from jax.experimental import pallas as pl
from jax.experimental.pallas import tpu as pltpu
from jax.sharding import PartitionSpec as P

NV = 32
GX = 32
WX = 4
Q = NV * NV
HALF = Q // 2
BATCHES = 2
OWN = 2
BLOCK = 2 * OWN
VEL = 16
SPACE = 8
ROWS = NV * OWN
FACTORS = 5
INPUTS = 17
courant = 0.12
top_speed = 4.0
collide_step = 0.5
MESH = pl.DeviceIdType.MESH
f32 = jnp.float32
bf16 = jnp.bfloat16


def parts_of(table):
    hi = table.astype(np.float32).astype(ml_dtypes.bfloat16)
    lo = (table - hi.astype(np.float64)).astype(np.float32).astype(ml_dtypes.bfloat16)
    return hi, lo


def class_slots(parity):
    seen, slots = set(), []
    for kj in range(parity, NV, 2):
        for kl in range(NV):
            other = ((-kj) % NV, (-kl) % NV)
            if other == (kj, kl) or (kj, kl) in seen:
                continue
            seen.add((kj, kl))
            seen.add(other)
            slots.append((kj, kl))
    return slots


def tables():
    j, l = np.divmod(np.arange(HALF), NV)

    def angle(k):
        return 2 * np.pi * ((k[0] * j + k[1] * l) % NV) / NV

    selfs = [((0, 0), (16, 0)), ((0, 16), (16, 16))]
    even, odd = class_slots(0), class_slots(1)
    pair = np.sqrt(2.0) / NV
    t_even = np.zeros((HALF, HALF))
    t_odd = np.zeros((HALF, HALF))
    quarter = HALF // 2
    for n, (a, b) in enumerate(selfs):
        t_even[:, n] = np.cos(angle(a)) / NV
        t_even[:, quarter + n] = np.cos(angle(b)) / NV
    for n, k in enumerate(even):
        t_even[:, n + 2] = pair * np.cos(angle(k))
        t_even[:, quarter + n + 2] = -pair * np.sin(angle(k))
    for n, k in enumerate(odd):
        t_odd[:, n] = pair * np.cos(angle(k))
        t_odd[:, quarter + n] = -pair * np.sin(angle(k))
    big = np.stack(parts_of(t_even) + parts_of(t_odd) + parts_of(t_even.T) + parts_of(t_odd.T))

    phase = 2 * np.pi * (np.outer(np.arange(NV), np.arange(NV)) % NV) / NV
    c = np.kron(np.cos(phase), np.eye(OWN))
    s = np.kron(np.sin(phase), np.eye(OWN))
    fwd = np.block([[c, s], [-s, c]])
    flip = np.block([[c, -s], [-s, -c]])
    inv = np.block([[c, -s], [s, c]])
    left = []
    for hi, lo in (parts_of(t) for t in (fwd, flip, inv)):
        left.append(np.block([[hi, hi], [lo, np.zeros_like(lo)]]))
    left = np.stack(left)

    w = 0.5 / NV
    width = HALF + 128
    pick = np.zeros((2, Q, width))

    def put(column, k, weight):
        pick[0, k[0] * NV + k[1], column] += weight
        pick[1, ((-k[0]) % NV) * NV + ((-k[1]) % NV), column] += weight

    for n, (a, b) in enumerate(selfs):
        put(n, a, w / 2)
        put(n, b, w / 2)
        put(HALF + n, a, w / 2)
        put(HALF + n, b, -w / 2)
    for n, k in enumerate(even):
        put(n + 2, k, w)
    for n, k in enumerate(odd):
        put(quarter + n, k, w)
    pick = np.concatenate([pick[0], pick[1]], axis=1).astype(ml_dtypes.bfloat16)

    row = np.kron(np.eye(NV), np.ones((OWN, 1)))
    back_row = row[:, (-np.arange(NV)) % NV]
    spread = np.concatenate([row, back_row, row, back_row], axis=1).astype(ml_dtypes.bfloat16)
    row_j = np.kron(np.eye(NV), np.ones((1, NV))).astype(ml_dtypes.bfloat16)
    row_l = np.kron(np.ones((1, NV)), np.eye(NV)).astype(ml_dtypes.bfloat16)
    return big, left, pick, spread, row.astype(ml_dtypes.bfloat16), np.ascontiguousarray(row.T).astype(
        ml_dtypes.bfloat16
    ), np.stack([row_j, row_l])


def split(x):
    hi = x.astype(bf16)
    return hi, (x - hi.astype(f32)).astype(bf16)


def dot(a, b):
    return jnp.dot(a, b, preferred_element_type=f32)


def dot_first(a, b):
    return lax.dot_general(a, b, (((0,), (0,)), ((), ())), preferred_element_type=f32)


def right3(x, table_hi, table_lo):
    hi, lo = x
    both = dot(jnp.concatenate([hi, lo], axis=0), table_hi)
    return both[: hi.shape[0]] + (both[hi.shape[0] :] + dot(hi, table_lo))


def left3(table, x):
    both = dot(table, jnp.concatenate(x, axis=0))
    count = table.shape[0] // 2
    return both[:count] + both[count:]


def kernel(*refs):
    given, (back, *scratch) = refs[:INPUTS], refs[INPUTS:]
    x_hbm = given[0]
    held, scratch = scratch[:INPUTS], scratch[INPUTS:]
    (
        xv,
        spec,
        pick,
        big,
        left,
        spread,
        row_out,
        row_in,
        lanes_in,
        normal,
        tangent,
        emitted,
        flags,
        slabs,
        species,
        blow,
        rates,
    ) = held
    (
        upper,
        lower,
        send,
        recv,
        result,
        spectrum,
        mirrored,
        spec_rows,
        weights,
        weights_self,
        wall_hi,
        wall_lo,
        part,
        grid_hi,
        grid_lo,
        load_sem,
        keep_sem,
        halo_send,
        halo_recv,
        near_send,
        near_recv,
        out_send,
        out_recv,
        back_send,
        back_recv,
    ) = scratch
    space = lax.axis_index("space")
    vel = lax.axis_index("vel")
    place_y, place_x, place_c = vel // 4, (vel // 2) % 2, vel % 2
    after, before = (space + 1) % SPACE, (space + SPACE - 1) % SPACE

    def peer(dy, dx, dc):
        return ((place_y + dy) % 4) * 4 + ((place_x + dx) % 2) * 2 + (place_c + dc) % 2

    offsets = [
        (dy, dx, dc)
        for dy in (2, 1, 3, 0)
        for dx in (1, 0)
        for dc in (1, 0)
        if (dy, dx, dc) != (0, 0, 0)
    ]

    barrier = pltpu.get_barrier_semaphore()
    for other in (after, before):
        pl.semaphore_signal(barrier, inc=1, device_id=(other, vel), device_id_type=MESH)
    for offset in offsets:
        pl.semaphore_signal(barrier, inc=1, device_id=(space, peer(*offset)), device_id_type=MESH)

    loads = [
        pltpu.make_async_copy(src, dst, load_sem.at[n]) for n, (src, dst) in enumerate(zip(given, held))
    ]
    loads[0].start()
    pl.semaphore_wait(barrier, VEL + 1)

    chunks = GX // 8

    def chunk(step):
        return 2 * (step // 2) + (step + place_y) % 2

    def halo(m, own, number):
        rows = pl.multiple_of(m * 8, 8)
        low = x_hbm.at[pl.ds(rows, 8), pl.ds(own * Q, HALF)]
        high = x_hbm.at[pl.ds(GX + rows, 8), pl.ds(own * Q + HALF, HALF)]
        src, dst, other = ((low, upper, before), (high, lower, after))[number]
        return pltpu.make_async_remote_copy(
            src_ref=src,
            dst_ref=dst.at[own, pl.ds(rows, 8)],
            send_sem=halo_send.at[number, own * chunks + m],
            recv_sem=halo_recv.at[number, own * chunks + m],
            device_id=(other, vel),
            device_id_type=MESH,
        )

    for t in range(chunks):
        for own in range(2):
            for number in range(2):
                halo(chunk(t), own, number).start()
    for load in loads[1:]:
        load.start()
    loads[0].wait()

    lane = lax.broadcasted_iota(jnp.int32, (1, HALF), 1)
    cell = lax.broadcasted_iota(jnp.int32, (GX, HALF), 0)

    def speed(index):
        return courant * ((2.0 * index.astype(f32) + 1.0 - NV) / NV * top_speed)

    def along_normal(group, half, own):
        at = own * Q + half * HALF
        f = xv[group * GX : (group + 1) * GX, at : at + HALF]
        wall_side = jnp.where(cell == 0, 0.0, pltpu.roll(f, 1, 0))
        far_side = jnp.where(cell == GX - 1, 0.0, pltpu.roll(f, GX - 1, 0))
        a = speed(vel * 2 + own)
        read = f - jnp.maximum(a, 0.0) * (f - wall_side)
        return f, read - jnp.minimum(a, 0.0) * (far_side - f)

    def along_wall(half, f, read, neighbour):
        return read - jnp.abs(speed((lane + half * HALF) // NV)) * (f - neighbour)

    def pack(group, m, lanes, r0, r1):
        for k in range(4):
            pair = slice(OWN * k, OWN * k + OWN)
            block = jnp.concatenate([r0[pair], r1[pair]], axis=0)
            send[m // 2, 8 * group + 4 * (m % 2) + k, :, lanes] = block

    def lanes_of(half):
        return pl.ds(pl.multiple_of(half * HALF, HALF), HALF)

    def near(owner, dest):
        lanes = lanes_of(dest // 8)
        return pltpu.make_async_remote_copy(
            src_ref=send.at[:, dest, :, lanes],
            dst_ref=recv.at[:, owner, :, lanes],
            send_sem=near_send.at[dest],
            recv_sem=near_recv.at[owner],
            device_id=(space, dest),
            device_id_type=MESH,
        )

    def far(batch, owner, dest):
        lanes = lanes_of(1 - dest // 8)
        return pltpu.make_async_remote_copy(
            src_ref=send.at[batch, dest, :, lanes],
            dst_ref=recv.at[batch, owner, :, lanes],
            send_sem=out_send.at[batch, dest],
            recv_sem=out_recv.at[batch, owner],
            device_id=(space, dest),
            device_id_type=MESH,
        )

    for group in range(2):
        half = group
        at = half * HALF
        other = slice((1 - group) * GX, (2 - group) * GX)
        read = []
        for own in range(2):
            f, along = along_normal(group, half, own)
            neighbour = xv[other, own * Q + at : own * Q + at + HALF]
            read.append(along_wall(half, f, along, neighbour))
        for m in range(chunks):
            pack(group, m, slice(at, at + HALF), *(r[8 * m : 8 * m + 8] for r in read))
    for offset in offsets:
        near(vel, peer(*offset)).start()

    for group in range(2):
        for own in range(2):
            part[group, own] = along_normal(group, 1 - group, own)[1]
    for load in loads[1:]:
        load.wait()
    zero3 = jnp.zeros((8 - FACTORS, Q), f32)
    for k in range(NV):
        spec_rows[k] = jnp.concatenate([spec[:, k * Q : (k + 1) * Q], zero3], axis=0)
    width = HALF + 128
    rows_hi, rows_lo = split(
        jnp.concatenate([spec_rows[:, r, :] for r in range(FACTORS)], axis=0)
    )
    both = dot(jnp.concatenate([rows_hi, rows_lo], axis=0), pick[...])
    both = split(both[: FACTORS * NV] + both[FACTORS * NV :])
    for r in range(FACTORS):
        pieces = [b[r * NV : (r + 1) * NV, n * width : (n + 1) * width] for b in both for n in range(2)]
        whole = dot(spread[...], jnp.concatenate(pieces, axis=0))
        weights[r] = whole[:, :HALF]
        weights_self[r] = whole[:, HALF:]

    def second_phase(t, carry):
        m = chunk(t)
        rows = pl.multiple_of(m * 8, 8)
        for own in range(2):
            for number in range(2):
                halo(m, own, number).wait_recv()
        for group in range(2):
            half = 1 - group
            at = half * HALF
            beside = (lower, upper)[group]
            read = []
            for own in range(2):
                f = xv[pl.ds(group * GX + rows, 8), own * Q + at : own * Q + at + HALF]
                along = part[group, own, pl.ds(rows, 8)]
                read.append(along_wall(half, f, along, beside[own, pl.ds(rows, 8)]))
            pack(group, m, slice(at, at + HALF), *read)
            for k in range(4):
                dest = 8 * group + 4 * (m % 2) + k

                @pl.when(dest != vel)
                def _():
                    far(m // 2, vel, dest).start()

        return carry

    for t in range(chunks):
        second_phase(t, 0)
    keep = pltpu.make_async_copy(send.at[:, vel], recv.at[:, vel], keep_sem.at[0])
    keep.start()

    row_id = lax.broadcasted_iota(jnp.int32, (ROWS, 1), 0) % OWN
    first_cell = (vel // 8) * GX + (vel % 8) * OWN
    wall_here = vel % 8 < WX // OWN
    kind = 0
    slab = 0
    for c in range(OWN):
        kind = kind + flags[first_cell + c] * species[first_cell + c]
        slab = slab + flags[first_cell + c] * slabs[first_cell + c]

    @pl.when(wall_here)
    def _():
        turn = split(jnp.where(kind == 1, tangent[1], tangent[0]))
        by_j = dot_first(turn[0], lanes_in[0]) + dot_first(turn[1], lanes_in[0])
        by_l = dot_first(turn[0], lanes_in[1]) + dot_first(turn[1], lanes_in[1])
        for j in range(NV):
            hi, lo = split(by_j[j : j + 1, :] * by_l)
            wall_hi[j * NV : (j + 1) * NV, :] = hi
            wall_lo[j * NV : (j + 1) * NV, :] = lo

    def home(batch, dest):
        return pltpu.make_async_remote_copy(
            src_ref=result.at[batch, dest],
            dst_ref=back.at[batch, vel],
            send_sem=back_send.at[batch, dest],
            recv_sem=back_recv.at[batch, vel],
            device_id=(space, dest),
            device_id_type=MESH,
        )

    def arrival(batch, owner):
        return pltpu.make_async_remote_copy(
            src_ref=result.at[batch, vel],
            dst_ref=back.at[batch, owner],
            send_sem=back_send.at[batch, owner],
            recv_sem=back_recv.at[batch, owner],
            device_id=(space, owner),
            device_id_type=MESH,
        )

    for offset in offsets:
        near(peer(*offset), vel).wait_recv()
    keep.wait()
    quarter = HALF // 2
    count = ROWS // 2

    def collide(batch, carry):
        for offset in offsets:
            far(batch, peer(*offset), vel).wait_recv()

        @pl.when(jnp.logical_and(wall_here, batch == 0))
        def _():
            scatter = split(jnp.where(kind == 1, normal[1], normal[0]))
            wide = split(dot(row_out[...], scatter[0]) + dot(row_out[...], scatter[1]))
            wide = dot(wide[0], row_in[...]) + dot(wide[1], row_in[...])
            same = row_id == lax.broadcasted_iota(jnp.int32, (1, ROWS), 1) % OWN
            wide = split(jnp.where(same, wide, 0.0))
            x = recv[0].reshape(ROWS, Q)
            turned = split(right3(split(x), wall_hi[...], wall_lo[...]))
            reflected = dot(wide[0], turned[0]) + (dot(wide[1], turned[0]) + dot(wide[0], turned[1]))
            gas = jnp.concatenate(
                [emitted[pl.ds(t, NV, stride=Q // 128), :] for t in range(Q // 128)], axis=1
            )
            gas = split(gas)
            gas = dot(row_out[...], gas[0]) + dot(row_out[...], gas[1])
            reflected = reflected + blow[slab] * gas
            flag_column = jnp.zeros((ROWS, 1), jnp.int32)
            for c in range(OWN):
                flag_column = jnp.where(row_id == c, flags[first_cell + c], flag_column)
            recv[0] = jnp.where(flag_column == 1, reflected, x).reshape(VEL, BLOCK, Q)

        rate_part = jnp.zeros((count, 1), f32)
        for c in range(OWN):
            kind_here = species[first_cell + batch * (GX // BATCHES) + c]
            rate = jnp.where(kind_here == 1, rates[1], rates[0])
            rate_part = jnp.where(row_id[:count] == c, collide_step * rate, rate_part)

        xa = recv[batch, :, :, :HALF].reshape(ROWS, HALF)
        xb = recv[batch, :, :, HALF:].reshape(ROWS, HALF)
        ye = right3(split(xa + xb), big[0], big[1])
        yo = right3(split(xa - xb), big[2], big[3])
        z = jnp.concatenate(
            [
                jnp.concatenate([ye[:, :quarter], yo[:, :quarter]], axis=1),
                jnp.concatenate([ye[:, quarter:], yo[:, quarter:]], axis=1),
            ],
            axis=0,
        )
        z = split(z)
        spectrum[...] = left3(left[0], z)
        mirrored[...] = left3(left[1], (z[0][:, :128], z[1][:, :128]))

        def weigh(r, carry):
            w = jnp.concatenate([weights[r], weights[r]], axis=0)
            d = jnp.concatenate([weights_self[r], weights_self[r]], axis=0)
            scaled = spectrum[...] * w
            first = scaled[:, :128] + mirrored[...] * d
            scaled = split(jnp.concatenate([first, scaled[:, 128:]], axis=1))
            hi, lo = split(left3(left[2], scaled))
            for part_, grid in ((hi, grid_hi), (lo, grid_lo)):
                for block in range(2):
                    lanes = slice(block * quarter, (block + 1) * quarter)
                    grid[block, r, :, :quarter] = part_[:ROWS, lanes]
                    grid[block, r, :, quarter:] = part_[ROWS:, lanes]
            return carry

        for r in range(FACTORS):
            weigh(r, 0)

        def restore(step, carry):
            side = (place_y // 2 + 1 + step) % 2
            rows = pl.ds(pl.multiple_of(side * count, count), count)
            sums = []
            for block in range(2):
                lhs = [
                    jnp.concatenate([grid[block, r, rows, :] for r in range(FACTORS)], axis=0)
                    for grid in (grid_hi, grid_lo)
                ]
                sums.append(right3(lhs, big[4 + 2 * block], big[5 + 2 * block]))
            owners = pl.ds(side * (VEL // 2), VEL // 2)
            for half, total in ((0, sums[0] + sums[1]), (1, sums[0] - sums[1])):
                filtered = [total[r * count : (r + 1) * count] for r in range(FACTORS)]
                lanes = slice(half * HALF, (half + 1) * HALF)
                walled = recv[batch, owners, :, lanes].reshape(count, HALF)
                gained = filtered[0] * filtered[2] + filtered[1] * filtered[3]
                updated = walled + rate_part * (gained - walled * filtered[4])
                result[batch, owners, :, lanes] = updated.reshape(VEL // 2, BLOCK, HALF)
            for plane in range(2):
                for dx in (1, 0):
                    for dc in (1, 0):
                        dest = (side * 2 + (place_y + plane) % 2) * 4
                        dest = dest + ((place_x + dx) % 2) * 2 + (place_c + dc) % 2

                        @pl.when(dest != vel)
                        def _():
                            home(batch, dest).start()

            return carry

        for step in range(2):
            restore(step, 0)
        return carry

    for batch in range(BATCHES):
        collide(batch, 0)
    keep = pltpu.make_async_copy(result.at[:, vel], back.at[:, vel], keep_sem.at[1])
    keep.start()

    for m in range(chunks):
        for own in range(2):
            for number in range(2):
                halo(m, own, number).wait_send()
    for offset in offsets:
        near(vel, peer(*offset)).wait_send()
        for batch in range(BATCHES):
            far(batch, vel, peer(*offset)).wait_send()
            home(batch, peer(*offset)).wait_send()
            arrival(batch, peer(*offset)).wait_recv()
    keep.wait()


def place(back, out, held, rows, load_sem, store_sem):
    loads, stores = [], []
    for n in range(GX // 4):
        group, m = n // 4, n % 4
        owners = (m // 2, pl.ds(8 * group + 4 * (m % 2), 4))
        cells = pl.ds(8 * n, 8)
        loads.append(pltpu.make_async_copy(back.at[owners], held.at[n], load_sem.at[n]))
        stores.append(pltpu.make_async_copy(rows.at[cells], out.at[cells], store_sem.at[n]))
        loads[n].start()
    for n in range(GX // 4):
        loads[n].wait()
        for own in range(2):
            block = [held[n, k, own * OWN : (own + 1) * OWN, :] for k in range(4)]
            rows[8 * n : 8 * n + 8, own * Q : (own + 1) * Q] = jnp.concatenate(block, axis=0)
        stores[n].start()
    for store in stores:
        store.wait()


def on_device(
    distribution,
    wall_flags,
    cell_slab,
    species,
    normal_kernel,
    tangent_kernel,
    blow_rate,
    emitted,
    spectral,
    collide_rate,
):
    big, left, pick, spread, row_out, row_in, lanes_in = (jnp.asarray(t) for t in tables())
    dma = pltpu.SemaphoreType.DMA
    in_vmem = [
        distribution,
        spectral,
        pick,
        big,
        left,
        spread,
        row_out,
        row_in,
        lanes_in,
        normal_kernel,
        tangent_kernel,
        emitted.reshape(NV * Q // 128, 128),
    ]
    in_smem = [wall_flags, cell_slab, species, blow_rate, collide_rate]
    back = pl.pallas_call(
        kernel,
        out_shape=jax.ShapeDtypeStruct((BATCHES, VEL, BLOCK, Q), f32),
        in_specs=[pl.BlockSpec(memory_space=pltpu.HBM)] * INPUTS,
        out_specs=pl.BlockSpec(memory_space=pltpu.HBM),
        scratch_shapes=[pltpu.VMEM(x.shape, x.dtype) for x in in_vmem]
        + [pltpu.SMEM(x.shape, x.dtype) for x in in_smem]
        + [
            pltpu.VMEM((2, GX, HALF), f32),
            pltpu.VMEM((2, GX, HALF), f32),
            pltpu.VMEM((BATCHES, VEL, BLOCK, Q), f32),
            pltpu.VMEM((BATCHES, VEL, BLOCK, Q), f32),
            pltpu.VMEM((BATCHES, VEL, BLOCK, Q), f32),
            pltpu.VMEM((2 * ROWS, HALF), f32),
            pltpu.VMEM((2 * ROWS, 128), f32),
            pltpu.VMEM((NV, 8, Q), f32),
            pltpu.VMEM((FACTORS, ROWS, HALF), f32),
            pltpu.VMEM((FACTORS, ROWS, 128), f32),
            pltpu.VMEM((Q, Q), bf16),
            pltpu.VMEM((Q, Q), bf16),
            pltpu.VMEM((2, 2, GX, HALF), f32),
            pltpu.VMEM((2, FACTORS, ROWS, HALF), bf16),
            pltpu.VMEM((2, FACTORS, ROWS, HALF), bf16),
            dma((INPUTS,)),
            dma((2,)),
            dma((2, 2 * GX // 8)),
            dma((2, 2 * GX // 8)),
            dma((VEL,)),
            dma((VEL,)),
            dma((BATCHES, VEL)),
            dma((BATCHES, VEL)),
            dma((BATCHES, VEL)),
            dma((BATCHES, VEL)),
        ],
        compiler_params=pltpu.CompilerParams(
            collective_id=0, has_side_effects=True, vmem_limit_bytes=56 * 2**20
        ),
        name="step",
    )(*in_vmem, *in_smem)
    return pl.pallas_call(
        place,
        out_shape=jax.ShapeDtypeStruct((2 * GX, 2 * Q), f32),
        in_specs=[pl.BlockSpec(memory_space=pltpu.HBM)],
        out_specs=pl.BlockSpec(memory_space=pltpu.HBM),
        scratch_shapes=[
            pltpu.VMEM((GX // 4, 4, BLOCK, Q), f32),
            pltpu.VMEM((2 * GX, 2 * Q), f32),
            dma((GX // 4,)),
            dma((GX // 4,)),
        ],
        compiler_params=pltpu.CompilerParams(vmem_limit_bytes=60 * 2**20),
        name="place",
    )(back)


def solution(mesh):
    in_specs = (P("space", "vel"), P("space"), P("space"), P("space"), P(), P(), P(), P(), P(), P())
    out_specs = P("space", "vel")
    return jax.shard_map(
        on_device, mesh=mesh, in_specs=in_specs, out_specs=out_specs, check_vma=False
    )
```
